256 devices in a mesh: sector: 16 (over y_lo, z), band: 16 (over y_hi, x, core).
Axes of the slice: x: 4, y: 4 (y_hi: 2, y_lo: 2; y = y_hi * 2 + y_lo), z: 8, core: 2. Of those that a mesh axis runs over, the one named last changes fastest.
Arguments:
- gas_density: bfloat16 [6144, 8192], P('band', 'sector'), may hold values from 0.29882812 to 3
- green_radial: bfloat16 [5, 6144, 1152], P(None, 'band'), may hold values from -0.1875 to 0.1875
- green_azimuth: bfloat16 [5, 512, 512], replicated, may hold values from -0.25 to 0.25
- dust_density: float32 [6144, 8192], P('band', 'sector'), may hold values from 0.2 to 2
- dust_radial_velocity: float32 [6144, 8192], P('band', 'sector'), may hold values from -1.5 to 1.5
- dust_azimuth_velocity: float32 [6144, 8192], P('band', 'sector'), may hold values from -1.5 to 1.5
- coupling: bfloat16 [6144, 8192], P('band', 'sector'), may hold values from 0.019897461 to 0.5
Outputs:
- potential: float32 [6144, 8192], P('band', 'sector')
- density_next: float32 [6144, 8192], P('band', 'sector')
- radial_next: float32 [6144, 8192], P('band', 'sector')
- azimuth_next: float32 [6144, 8192], P('band', 'sector')
The draws below stay inside these ranges and needn't reach their ends.
All inputs are finite; a program needn't handle non-finite values.
Results may differ from the reference program's by a relative error of at most 0.0028.
Values may be sent and summed in bfloat16 or wider, within the bound.
A program may use at most 128 MiB of HBM per device.

```python
import math
import jax
import jax.numpy as jnp
from jax import lax

ROWS = 384
ARC = 512
NR = 6144
NPHI = 8192


def levels(own_key, shape, pieces, least, high):
    loudness, own = 1.0, jax.random.fold_in(own_key, 6)
    for position, shards_of in pieces:
        draws = jnp.exp(jax.random.uniform(jax.random.fold_in(own, position), (shards_of,), jnp.float32, least / len(pieces), high / len(pieces)))
        loudness = loudness * jnp.repeat(draws, shape[position] // shards_of).reshape([-1 if axis == position else 1 for axis in range(len(shape))])
    return loudness


def centred(stream_key, extent, deviation, bound, pieces=(), kind=jnp.bfloat16):
    factor_of = levels(stream_key, extent, pieces, -0.22, 0.18) if pieces else 1.0
    values = jax.random.normal(stream_key, extent, jnp.float32) * deviation * factor_of
    return jnp.minimum(jnp.maximum(values, -bound), bound).astype(kind)


def setup_inputs(seed: int = 0) -> dict:
    seeds = jax.random.split(jax.random.key(seed), 8)
    return {
        "gas_density": jnp.clip(jnp.exp(math.log(3.0) - 2.306499 * jax.random.uniform(seeds[0], (NR, NPHI), jnp.float32) ** levels(seeds[0], (NR, NPHI), ((0, 16), (1, 16)), -0.2, 0.2)), 0.29882812, 3.0).astype(jnp.bfloat16),
        "green_radial": centred(seeds[1], (5, NR, 3 * ROWS), (3 * ROWS) ** -0.5, 0.1875, ((1, 16),)),
        "green_azimuth": centred(seeds[2], (5, ARC, ARC), ARC ** -0.5, 0.25),
        "dust_density": jnp.clip(jnp.exp(math.log(2.0) - 2.3025851 * jax.random.uniform(seeds[3], (NR, NPHI), jnp.float32) ** levels(seeds[3], (NR, NPHI), ((0, 16), (1, 16)), -0.2, 0.2)), 0.2, 2.0),
        "dust_radial_velocity": centred(seeds[4], (NR, NPHI), 0.3, 1.5, ((0, 16), (1, 16)), jnp.float32),
        "dust_azimuth_velocity": centred(seeds[5], (NR, NPHI), 0.3, 1.5, ((0, 16), (1, 16)), jnp.float32),
        "coupling": jnp.clip(jnp.exp(math.log(0.5) - 3.224016 * jax.random.uniform(seeds[6], (NR, NPHI), jnp.float32) ** levels(seeds[6], (NR, NPHI), ((0, 16), (1, 16)), -0.2, 0.2)), 0.019897461, 0.5).astype(jnp.bfloat16),
    }


diffusion = 0.1
gravity = 0.1
kepler = 0.6

def advance_dust(centre, upper_rows, lower_rows, east_side, west_side, potential_up, potential_down, potential_east, potential_west, coupling_rate, inv_radius):
    density = centre[0]
    radial = centre[1]
    azimuth = centre[2]
    laplace = upper_rows + lower_rows + east_side + west_side - 4.0 * centre
    flux_up = upper_rows[0] * upper_rows[1]
    flux_down = lower_rows[0] * lower_rows[1]
    flux_east = east_side[0] * east_side[2]
    flux_west = west_side[0] * west_side[2]
    gas_speed = kepler * jnp.sqrt(inv_radius)
    density_next = density - 0.5 * (flux_up - flux_down) - 0.5 * inv_radius * (flux_east - flux_west) + diffusion * laplace[0]
    radial_next = radial - 0.5 * radial * (upper_rows[1] - lower_rows[1]) - 0.5 * inv_radius * azimuth * (east_side[1] - west_side[1]) - 0.5 * gravity * (potential_up - potential_down) - coupling_rate * radial + diffusion * laplace[1]
    azimuth_next = azimuth - 0.5 * radial * (upper_rows[2] - lower_rows[2]) - 0.5 * inv_radius * azimuth * (east_side[2] - west_side[2]) - 0.5 * gravity * inv_radius * (potential_east - potential_west) - coupling_rate * (azimuth - gas_speed) + diffusion * laplace[2]
    return (density_next, radial_next, azimuth_next)

def reference(gas_density, green_radial, green_azimuth, dust_density, dust_radial_velocity, dust_azimuth_velocity, coupling):
    sector_count = NPHI // ARC
    band_count = NR // ROWS
    padded = jnp.pad(gas_density, ((ROWS, ROWS), (0, 0)))

    def one_band(band_index):
        window = lax.dynamic_slice_in_dim(padded, band_index * ROWS, 3 * ROWS, 0)
        weights = lax.dynamic_slice_in_dim(green_radial, band_index * ROWS, ROWS, 1)
        summed = jnp.zeros((ROWS, NPHI), jnp.float32)
        for offset in range(-2, 3):
            rolled = jnp.roll(window, offset * ARC, axis=1)
            radial = jnp.dot(weights[offset + 2], rolled, preferred_element_type=jnp.float32).astype(jnp.bfloat16)
            summed = summed + jnp.dot(radial.reshape(ROWS * sector_count, ARC), green_azimuth[offset + 2], preferred_element_type=jnp.float32).reshape(ROWS, NPHI)
        return summed
    potential = lax.map(one_band, jnp.arange(band_count, dtype=jnp.int32)).reshape(NR, NPHI)
    fields = jnp.stack([dust_density, dust_radial_velocity, dust_azimuth_velocity])
    upper_rows = jnp.pad(fields[:, 1:], ((0, 0), (0, 1), (0, 0)))
    lower_rows = jnp.pad(fields[:, :-1], ((0, 0), (1, 0), (0, 0)))
    east_side = jnp.roll(fields, -1, axis=2)
    west_side = jnp.roll(fields, 1, axis=2)
    potential_up = jnp.pad(potential[1:], ((0, 1), (0, 0)))
    potential_down = jnp.pad(potential[:-1], ((1, 0), (0, 0)))
    potential_east = jnp.roll(potential, -1, axis=1)
    potential_west = jnp.roll(potential, 1, axis=1)
    inv_radius = (1.0 / (1.0 + 3.0 * (jnp.arange(NR, dtype=jnp.float32) + 0.5) / NR))[:, None]
    density_next, radial_next, azimuth_next = advance_dust(fields, upper_rows, lower_rows, east_side, west_side, potential_up, potential_down, potential_east, potential_west, coupling.astype(jnp.float32), inv_radius)
    return (potential, density_next, radial_next, azimuth_next)
```

```python
import functools

import jax
import jax.numpy as jnp
from jax import lax
from jax.experimental import pallas as pl
from jax.experimental.pallas import tpu as pltpu
from jax.sharding import PartitionSpec as P

diffusion = 0.1
gravity = 0.1
kepler = 0.6

MESH = pl.DeviceIdType.MESH
F32 = jnp.float32
BF16 = jnp.bfloat16


def kernel(
    chunk,
    strip,
    gas,
    green_radial,
    green_azimuth,
    dust_density,
    dust_radial,
    dust_azimuth,
    coupling,
    potential,
    density_next,
    radial_next,
    azimuth_next,
    ext,
    gr,
    ga,
    fld,
    kv,
    potp,
    near,
    far_out,
    far_in,
    part_out,
    part_in,
    dcol_out,
    dcol_in,
    dcol,
    pcol_out,
    pcol_in,
    pcol,
    load_sem,
    gas_send,
    gas_recv,
    drow_send,
    drow_recv,
    dcol_send,
    dcol_recv,
    far_send,
    far_recv,
    part_send,
    part_recv,
    prow_send,
    prow_recv,
    pcol_send,
    pcol_recv,
):
    rows, arc = dust_density.shape
    chunks = rows // chunk
    band = lax.axis_index("band")
    sector = lax.axis_index("sector")
    bands = lax.axis_size("band")
    sectors = lax.axis_size("sector")
    ahead = lax.rem(sector + 1, sectors)
    behind = lax.rem(sector + sectors - 1, sectors)
    has_up = band < bands - 1
    has_down = band > 0
    side = (ahead, behind)

    def load(src, dst, n):
        copy = pltpu.make_async_copy(src, dst, load_sem.at[n])
        copy.start()
        return copy

    own = pl.ds(rows, rows)
    body_rows = pl.ds(8, rows)
    load_fields = [
        load(field, fld.at[n, body_rows, :], n)
        for n, field in enumerate((dust_density, dust_radial, dust_azimuth))
    ]
    load_gas = load(gas, ext.at[own, :], 3)
    load_gr = {}
    for n, j in enumerate((4, 0, 2, 3, 1)):
        load_gr[j] = load(green_radial.at[j], gr.at[j], 4 + n)
    load_ga = load(green_azimuth, ga, 9)
    load_k = load(coupling, kv, 10)

    barrier = pltpu.get_barrier_semaphore()
    for s in side:
        pl.semaphore_signal(barrier, inc=1, device_id={"sector": s}, device_id_type=MESH)

    @pl.when(has_up)
    def _():
        pl.semaphore_signal(barrier, inc=1, device_id={"band": band + 1}, device_id_type=MESH)

    @pl.when(has_down)
    def _():
        pl.semaphore_signal(barrier, inc=1, device_id={"band": band - 1}, device_id_type=MESH)

    pl.semaphore_wait(
        barrier, 2 + has_up.astype(jnp.int32) + has_down.astype(jnp.int32)
    )

    def remote(src, dst, send, recv, where):
        return pltpu.make_async_remote_copy(
            src_ref=src,
            dst_ref=dst,
            send_sem=send,
            recv_sem=recv,
            device_id=where,
            device_id_type=MESH,
        )

    up = {"band": band + 1}
    down = {"band": band - 1}
    gas_up = remote(gas, ext.at[pl.ds(0, rows), :], gas_send.at[0], gas_recv.at[0], up)
    gas_down = remote(gas, ext.at[pl.ds(2 * rows, rows), :], gas_send.at[1], gas_recv.at[1], down)
    top = pl.ds(rows, 8)
    bottom = pl.ds(8, 8)
    halo_low = pl.ds(0, 8)
    halo_high = pl.ds(rows + 8, 8)
    drow_up = remote(
        fld.at[:, top, :], fld.at[:, halo_low, :], drow_send.at[0], drow_recv.at[0], up
    )
    drow_down = remote(
        fld.at[:, bottom, :], fld.at[:, halo_high, :], drow_send.at[1], drow_recv.at[1], down
    )
    prow_up = remote(
        potp.at[top, :], potp.at[halo_low, :], prow_send.at[0], prow_recv.at[0], up
    )
    prow_down = remote(
        potp.at[bottom, :], potp.at[halo_high, :], prow_send.at[1], prow_recv.at[1], down
    )

    @pl.when(has_up)
    def _():
        gas_up.start()

    @pl.when(has_down)
    def _():
        gas_down.start()

    @pl.when(jnp.logical_not(has_down))
    def _():
        ext[0:rows, :] = jnp.zeros((rows, arc), BF16)
        fld[:, 0:8, :] = jnp.zeros((3, 8, arc), F32)
        potp[0:8, :] = jnp.zeros((8, arc), F32)

    @pl.when(jnp.logical_not(has_up))
    def _():
        ext[2 * rows : 3 * rows, :] = jnp.zeros((rows, arc), BF16)
        fld[:, rows + 8 : rows + 16, :] = jnp.zeros((3, 8, arc), F32)
        potp[rows + 8 : rows + 16, :] = jnp.zeros((8, arc), F32)

    for copy in load_fields:
        copy.wait()

    @pl.when(has_up)
    def _():
        drow_up.start()

    @pl.when(has_down)
    def _():
        drow_down.start()

    for d, first in ((0, arc - 128), (1, 0)):
        lane = 127 if d == 0 else 0
        for n in range(3):
            turned = jnp.transpose(fld[n, 8 : 8 + rows, first : first + 128])
            dcol_out[d, n : n + 1, :] = turned[lane : lane + 1, :]
        dcol_out[d, 3:8, :] = jnp.zeros((5, rows), F32)
    dcol_copies = [
        remote(
            dcol_out.at[d], dcol_in.at[d], dcol_send.at[d], dcol_recv.at[d], {"sector": side[d]}
        )
        for d in range(2)
    ]
    for copy in dcol_copies:
        copy.start()

    def far_copy(d, c):
        part = pl.ds(pl.multiple_of(c * chunk, chunk), chunk)
        return remote(
            far_out.at[d, part, :],
            far_in.at[d, part, :],
            far_send.at[d, c],
            far_recv.at[d, c],
            {"sector": side[d]},
        )

    def part_copy(d, c):
        part = pl.ds(pl.multiple_of(c * chunk, chunk), chunk)
        return remote(
            part_out.at[d, part, :],
            part_in.at[d, part, :],
            part_send.at[d, c],
            part_recv.at[d, c],
            {"sector": side[d]},
        )

    def pcol_copy(d, c):
        return remote(
            pcol_out.at[d, c],
            pcol_in.at[d, c],
            pcol_send.at[d, c],
            pcol_recv.at[d, c],
            {"sector": side[d]},
        )

    def nth(step):
        return lax.rem(chunks - step, chunks)

    load_gas.wait()
    load_gr[4].wait()
    load_gr[0].wait()

    @pl.when(has_up)
    def _():
        gas_up.wait_send()
        gas_down.wait_recv()

    @pl.when(has_down)
    def _():
        gas_down.wait_send()
        gas_up.wait_recv()

    @pl.loop(0, chunks)
    def _(step):
        c = nth(step)
        part = pl.ds(pl.multiple_of(c * chunk, chunk), chunk)
        for d, j in ((0, 4), (1, 0)):
            far_out[d, part, :] = jnp.dot(
                gr[j, part, :], ext[...], preferred_element_type=F32
            ).astype(BF16)
            far_copy(d, c).start()

    for j in (2, 3, 1):
        load_gr[j].wait()
    load_ga.wait()

    @pl.loop(0, chunks)
    def _(step):
        c = nth(step)
        part = pl.ds(pl.multiple_of(c * chunk, chunk), chunk)
        for d, j in ((0, 3), (1, 1)):
            near[d, part, :] = jnp.dot(
                gr[j, part, :], ext[...], preferred_element_type=F32
            ).astype(BF16)

    @pl.loop(0, chunks)
    def _(step):
        c = nth(step)
        part = pl.ds(pl.multiple_of(c * chunk, chunk), chunk)
        for d, j in ((0, 3), (1, 1)):
            close = jnp.dot(near[d, part, :], ga[j], preferred_element_type=F32)
            far_copy(d, c).wait_recv()
            total = close + jnp.dot(
                far_in[d, part, :], ga[4 - 4 * d], preferred_element_type=F32
            )
            part_out[d, part, :] = total.astype(BF16)
            part_copy(d, c).start()

    @pl.loop(0, chunks)
    def _(step):
        c = nth(step)
        part = pl.ds(pl.multiple_of(c * chunk, chunk), chunk)
        mid = jnp.dot(gr[2, part, :], ext[...], preferred_element_type=F32).astype(BF16)
        potential[part, :] = jnp.dot(mid, ga[2], preferred_element_type=F32)

    load_k.wait()
    for copy in dcol_copies:
        copy.wait()

    @pl.when(has_up)
    def _():
        drow_up.wait_send()
        drow_down.wait_recv()

    @pl.when(has_down)
    def _():
        drow_down.wait_send()
        drow_up.wait_recv()

    for d in range(2):
        dcol[d] = jnp.transpose(
            jnp.concatenate([dcol_in[d], jnp.zeros((120, rows), F32)], axis=0)
        )

    total_rows = rows * bands

    def inverse_radius(first, count):
        index = first + lax.broadcasted_iota(jnp.int32, (count, 1), 0)
        return 1.0 / (1.0 + 3.0 * (index.astype(F32) + 0.5) / total_rows)

    lanes = lax.broadcasted_iota(jnp.int32, (strip, arc), 1)
    is_first = lanes == 0
    is_last = lanes == arc - 1

    @pl.loop(0, rows // strip)
    def _(step):
        first = pl.multiple_of(step * strip, strip)
        part = pl.ds(first, strip)
        window = pl.ds(first, strip + 16)
        inv = inverse_radius(band * rows + first, strip)
        west_edge = dcol[0, part, :]
        east_edge = dcol[1, part, :]
        centre, above, below, east, west = [], [], [], [], []
        for n in range(3):
            q = fld[n, window, :]
            mid = q[8 : 8 + strip]
            centre.append(mid)
            above.append(q[9 : 9 + strip])
            below.append(q[7 : 7 + strip])
            east.append(jnp.where(is_last, east_edge[:, n : n + 1], pltpu.roll(mid, arc - 1, 1)))
            west.append(jnp.where(is_first, west_edge[:, n : n + 1], pltpu.roll(mid, 1, 1)))
        rho, u, w = centre
        k = kv[part, :].astype(F32)
        lap = [above[n] + below[n] + east[n] + west[n] - 4.0 * centre[n] for n in range(3)]
        density_next[part, :] = (
            rho
            - 0.5 * (above[0] * above[1] - below[0] * below[1])
            - 0.5 * inv * (east[0] * east[2] - west[0] * west[2])
            + diffusion * lap[0]
        )
        radial_next[part, :] = (
            u
            - 0.5 * u * (above[1] - below[1])
            - 0.5 * inv * w * (east[1] - west[1])
            - k * u
            + diffusion * lap[1]
        )
        azimuth_next[part, :] = (
            w
            - 0.5 * u * (above[2] - below[2])
            - 0.5 * inv * w * (east[2] - west[2])
            - k * (w - kepler * jnp.sqrt(inv))
            + diffusion * lap[2]
        )

    @pl.loop(0, chunks)
    def _(step):
        c = nth(step)
        part = pl.ds(pl.multiple_of(c * chunk, chunk), chunk)
        for d in range(2):
            part_copy(d, c).wait_recv()
        total = potential[part, :] + (part_in[0, part, :].astype(F32) + part_in[1, part, :].astype(F32))
        potential[part, :] = total
        potp[pl.ds(pl.multiple_of(c * chunk + 8, 8), chunk), :] = total
        for d, first in ((0, arc - 128), (1, 0)):
            lane = 127 if d == 0 else 0
            turned = jnp.transpose(total[:, first : first + 128])
            pcol_out[d, c, 0:1, :] = turned[lane : lane + 1, :]
            pcol_copy(d, c).start()

        @pl.when(jnp.logical_and(c == chunks - 1, has_up))
        def _():
            prow_up.start()

        @pl.when(jnp.logical_and(c == 0, has_down))
        def _():
            prow_down.start()

    @pl.when(has_up)
    def _():
        prow_up.wait_send()
        prow_down.wait_recv()

    @pl.when(has_down)
    def _():
        prow_down.wait_send()
        prow_up.wait_recv()

    lanes_c = lax.broadcasted_iota(jnp.int32, (chunk, arc), 1)
    first_c = lanes_c == 0
    last_c = lanes_c == arc - 1

    @pl.loop(0, chunks)
    def _(step):
        c = nth(step)
        first = pl.multiple_of(c * chunk, chunk)
        part = pl.ds(first, chunk)
        window = pl.ds(first, chunk + 16)
        inv = inverse_radius(band * rows + first, chunk)
        q = potp[window, :]
        mid = q[8 : 8 + chunk]
        for d in range(2):
            pcol_copy(d, c).wait()
            far_copy(d, c).wait_send()
            part_copy(d, c).wait_send()
        edges = []
        for d in range(2):
            full = jnp.concatenate([pcol_in[d, c], jnp.zeros((120, chunk), F32)], axis=0)
            edges.append(jnp.transpose(full)[:, 0:1])
        east = jnp.where(last_c, edges[1], pltpu.roll(mid, arc - 1, 1))
        west = jnp.where(first_c, edges[0], pltpu.roll(mid, 1, 1))
        radial_next[part, :] = radial_next[part, :] - 0.5 * gravity * (
            q[9 : 9 + chunk] - q[7 : 7 + chunk]
        )
        azimuth_next[part, :] = azimuth_next[part, :] - 0.5 * gravity * inv * (east - west)


def body(gas, green_radial, green_azimuth, rho, u, w, coupling, chunk, strip):
    rows, arc = rho.shape
    chunks = rows // chunk
    dma = pltpu.SemaphoreType.DMA
    out = [pltpu.VMEM((rows, arc), F32)] * 4
    return pl.pallas_call(
        functools.partial(kernel, chunk, strip),
        out_shape=out,
        in_specs=[pl.BlockSpec(memory_space=pl.ANY)] * 7,
        out_specs=[pl.BlockSpec(memory_space=pltpu.VMEM)] * 4,
        scratch_shapes=[
            pltpu.VMEM((3 * rows, arc), BF16),
            pltpu.VMEM((5, rows, 3 * rows), BF16),
            pltpu.VMEM((5, arc, arc), BF16),
            pltpu.VMEM((3, rows + 16, arc), F32),
            pltpu.VMEM((rows, arc), BF16),
            pltpu.VMEM((rows + 16, arc), F32),
            pltpu.VMEM((2, rows, arc), BF16),
            pltpu.VMEM((2, rows, arc), BF16),
            pltpu.VMEM((2, rows, arc), BF16),
            pltpu.VMEM((2, rows, arc), BF16),
            pltpu.VMEM((2, rows, arc), BF16),
            pltpu.VMEM((2, 8, rows), F32),
            pltpu.VMEM((2, 8, rows), F32),
            pltpu.VMEM((2, rows, 128), F32),
            pltpu.VMEM((2, chunks, 8, chunk), F32),
            pltpu.VMEM((2, chunks, 8, chunk), F32),
            pltpu.VMEM((2, rows, 128), F32),
            dma((11,)),
            dma((2,)),
            dma((2,)),
            dma((2,)),
            dma((2,)),
            dma((2,)),
            dma((2,)),
            dma((2, chunks)),
            dma((2, chunks)),
            dma((2, chunks)),
            dma((2, chunks)),
            dma((2,)),
            dma((2,)),
            dma((2, chunks)),
            dma((2, chunks)),
        ],
        compiler_params=pltpu.CompilerParams(
            collective_id=0, has_side_effects=True, vmem_limit_bytes=56 * 2**20
        ),
        name="disc",
    )(gas, green_radial, green_azimuth, rho, u, w, coupling)


def solution(mesh, chunk=128, strip=32):
    return jax.shard_map(
        functools.partial(body, chunk=chunk, strip=strip),
        mesh=mesh,
        in_specs=(
            P("band", "sector"),
            P(None, "band", None),
            P(),
            P("band", "sector"),
            P("band", "sector"),
            P("band", "sector"),
            P("band", "sector"),
        ),
        out_specs=(P("band", "sector"),) * 4,
        check_vma=False,
    )
```

```python
import functools

import jax
import jax.numpy as jnp
from jax import lax
from jax.experimental import pallas as pl
from jax.experimental.pallas import tpu as pltpu
from jax.sharding import PartitionSpec as P

diffusion = 0.1
gravity = 0.1
kepler = 0.6

MESH = pl.DeviceIdType.MESH
F32 = jnp.float32
BF16 = jnp.bfloat16


def kernel(
    chunk,
    strip,
    pieces,
    gas,
    green_radial,
    green_azimuth,
    dust_density,
    dust_radial,
    dust_azimuth,
    coupling,
    potential,
    density_next,
    radial_next,
    azimuth_next,
    ext,
    gr,
    ga,
    fld,
    kv,
    potp,
    near,
    far_out,
    far_in,
    part_out,
    part_in,
    col_out,
    col_in,
    col_own,
    dcol,
    load_sem,
    gas_send,
    gas_recv,
    row_send,
    row_recv,
    col_send,
    col_recv,
    far_send,
    far_recv,
    part_send,
    part_recv,
):
    rows, arc = dust_density.shape
    chunks = rows // chunk
    band = lax.axis_index("band")
    sector = lax.axis_index("sector")
    bands = lax.axis_size("band")
    sectors = lax.axis_size("sector")
    side = (lax.rem(sector + 1, sectors), lax.rem(sector + sectors - 1, sectors))
    side_two = (lax.rem(sector + 2, sectors), lax.rem(sector + sectors - 2, sectors))
    has_up = band < bands - 1
    has_down = band > 0

    def load(src, dst, n):
        copy = pltpu.make_async_copy(src, dst, load_sem.at[n])
        copy.start()
        return copy

    own = pl.ds(rows, rows)
    body_rows = pl.ds(8, rows)
    load_gas = load(gas, ext.at[own, :], 3)
    load_gr = {}
    for n, j in enumerate((4, 0)):
        load_gr[j] = load(green_radial.at[j], gr.at[j], 4 + n)
    load_fields = [
        load(field, fld.at[n, body_rows, :], n)
        for n, field in enumerate((dust_density, dust_radial, dust_azimuth))
    ]
    for n, j in enumerate((3, 1)):
        load_gr[j] = load(green_radial.at[j], gr.at[j], 6 + n)
    load_ga = load(green_azimuth, ga, 9)
    load_gr[2] = load(green_radial.at[2], gr.at[2], 8)
    load_k = load(coupling, kv, 10)

    barrier = pltpu.get_barrier_semaphore()
    for s in side + side_two:
        pl.semaphore_signal(barrier, inc=1, device_id={"sector": s}, device_id_type=MESH)

    @pl.when(has_up)
    def _():
        pl.semaphore_signal(barrier, inc=1, device_id={"band": band + 1}, device_id_type=MESH)

    @pl.when(has_down)
    def _():
        pl.semaphore_signal(barrier, inc=1, device_id={"band": band - 1}, device_id_type=MESH)

    pl.semaphore_wait(barrier, 4 + has_up.astype(jnp.int32) + has_down.astype(jnp.int32))

    def remote(src, dst, send, recv, where):
        return pltpu.make_async_remote_copy(
            src_ref=src,
            dst_ref=dst,
            send_sem=send,
            recv_sem=recv,
            device_id=where,
            device_id_type=MESH,
        )

    up = {"band": band + 1}
    down = {"band": band - 1}

    def gas_copies(n):
        cols = pl.ds(*pieces[n])
        return (
            remote(
                gas.at[:, cols],
                ext.at[pl.ds(0, rows), cols],
                gas_send.at[0, n],
                gas_recv.at[0, n],
                up,
            ),
            remote(
                gas.at[:, cols],
                ext.at[pl.ds(2 * rows, rows), cols],
                gas_send.at[1, n],
                gas_recv.at[1, n],
                down,
            ),
        )

    def start_both(copies):
        @pl.when(has_up)
        def _():
            copies[0].start()

        @pl.when(has_down)
        def _():
            copies[1].start()

    def wait_both(copies):
        @pl.when(has_up)
        def _():
            copies[0].wait_send()
            copies[1].wait_recv()

        @pl.when(has_down)
        def _():
            copies[1].wait_send()
            copies[0].wait_recv()

    for n in range(len(pieces)):
        start_both(gas_copies(n))

    top = pl.ds(rows, 8)
    bottom = pl.ds(8, 8)
    halo_low = pl.ds(0, 8)
    halo_high = pl.ds(rows + 8, 8)
    drow = (
        remote(fld.at[:, top, :], fld.at[:, halo_low, :], row_send.at[0], row_recv.at[0], up),
        remote(fld.at[:, bottom, :], fld.at[:, halo_high, :], row_send.at[1], row_recv.at[1], down),
    )
    prow = (
        remote(potp.at[top, :], potp.at[halo_low, :], row_send.at[2], row_recv.at[2], up),
        remote(potp.at[bottom, :], potp.at[halo_high, :], row_send.at[3], row_recv.at[3], down),
    )

    @pl.when(jnp.logical_not(has_down))
    def _():
        ext[0:rows, :] = jnp.zeros((rows, arc), BF16)
        fld[:, 0:8, :] = jnp.zeros((3, 8, arc), F32)
        potp[0:8, :] = jnp.zeros((8, arc), F32)

    @pl.when(jnp.logical_not(has_up))
    def _():
        ext[2 * rows : 3 * rows, :] = jnp.zeros((rows, arc), BF16)
        fld[:, rows + 8 : rows + 16, :] = jnp.zeros((3, 8, arc), F32)
        potp[rows + 8 : rows + 16, :] = jnp.zeros((8, arc), F32)

    def col_copy(kind, d):
        where = side_two[d] if kind == 2 else side[d]
        return remote(
            col_out.at[kind, d],
            col_in.at[kind, d],
            col_send.at[kind, d],
            col_recv.at[kind, d],
            {"sector": where},
        )

    def edge(tile, d):
        lane = 127 if d == 0 else 0
        return jnp.transpose(tile)[lane : lane + 1, :]

    def edge_tile(d):
        return slice(arc - 128, arc) if d == 0 else slice(0, 128)

    for copy in load_fields:
        copy.wait()
    start_both(drow)
    for d in range(2):
        for n in range(3):
            col_out[0, d, n : n + 1, :] = edge(fld[n, 8 : 8 + rows, edge_tile(d)], d)
        col_copy(0, d).start()

    def far_copy(d, n):
        if n < len(pieces) - 1:
            part, cols = pl.ds(0, rows), pl.ds(*pieces[n])
        else:
            c = n - (len(pieces) - 1)
            part, cols = pl.ds(c * chunk, chunk), pl.ds(*pieces[-1])
        return remote(
            far_out.at[d, part, cols],
            far_in.at[d, part, cols],
            far_send.at[d, n],
            far_recv.at[d, n],
            {"sector": side[d]},
        )

    def part_copy(d, c):
        part = pl.ds(c * chunk, chunk)
        return remote(
            part_out.at[d, part, :],
            part_in.at[d, part, :],
            part_send.at[d, c],
            part_recv.at[d, c],
            {"sector": side[d]},
        )

    order = [(chunks - n) % chunks for n in range(chunks)]
    whole = len(pieces) - 1
    load_gas.wait()
    load_gr[4].wait()
    load_gr[0].wait()
    for n in range(whole):
        wait_both(gas_copies(n))
        cols = slice(pieces[n][0], pieces[n][0] + pieces[n][1])
        for d, j in ((0, 4), (1, 0)):
            far_out[d, :, cols] = jnp.dot(
                gr[j], ext[:, cols], preferred_element_type=F32
            ).astype(BF16)
            far_copy(d, n).start()
    wait_both(gas_copies(whole))
    last = slice(pieces[-1][0], arc)
    for c in order:
        part = slice(c * chunk, (c + 1) * chunk)
        for d, j in ((0, 4), (1, 0)):
            far_out[d, part, last] = jnp.dot(
                gr[j, part, :], ext[:, last], preferred_element_type=F32
            ).astype(BF16)
            far_copy(d, whole + c).start()

    load_gr[3].wait()
    load_gr[1].wait()
    load_ga.wait()
    for d, j in ((0, 3), (1, 1)):
        near[d] = jnp.dot(gr[j], ext[...], preferred_element_type=F32).astype(BF16)

    load_k.wait()
    for d in range(2):
        col_copy(0, d).wait()
    wait_both(drow)

    def columns(block):
        return jnp.transpose(jnp.concatenate([block, jnp.zeros((120, rows), F32)], axis=0))

    for d in range(2):
        dcol[d] = columns(col_in[0, d])

    total_rows = rows * bands

    def inverse_radius(first, count):
        index = first + lax.broadcasted_iota(jnp.int32, (count, 1), 0)
        return 1.0 / (1.0 + 3.0 * (index.astype(F32) + 0.5) / total_rows)

    def dust(start, stop):
        lanes = lax.broadcasted_iota(jnp.int32, (strip, arc), 1)
        is_first = lanes == 0
        is_last = lanes == arc - 1

        @pl.loop(start // strip, stop // strip)
        def _(step):
            first = pl.multiple_of(step * strip, strip)
            part = pl.ds(first, strip)
            window = pl.ds(first, strip + 16)
            inv = inverse_radius(band * rows + first, strip)
            west_edge = dcol[0, part, :]
            east_edge = dcol[1, part, :]
            centre, above, below, east, west = [], [], [], [], []
            for n in range(3):
                q = fld[n, window, :]
                mid = q[8 : 8 + strip]
                centre.append(mid)
                above.append(q[9 : 9 + strip])
                below.append(q[7 : 7 + strip])
                east.append(
                    jnp.where(is_last, east_edge[:, n : n + 1], pltpu.roll(mid, arc - 1, 1))
                )
                west.append(jnp.where(is_first, west_edge[:, n : n + 1], pltpu.roll(mid, 1, 1)))
            rho, u, w = centre
            k = kv[part, :].astype(F32)
            lap = [above[n] + below[n] + east[n] + west[n] - 4.0 * centre[n] for n in range(3)]
            density_next[part, :] = (
                rho
                - 0.5 * (above[0] * above[1] - below[0] * below[1])
                - 0.5 * inv * (east[0] * east[2] - west[0] * west[2])
                + diffusion * lap[0]
            )
            radial_next[part, :] = (
                u
                - 0.5 * u * (above[1] - below[1])
                - 0.5 * inv * w * (east[1] - west[1])
                - k * u
                + diffusion * lap[1]
            )
            azimuth_next[part, :] = (
                w
                - 0.5 * u * (above[2] - below[2])
                - 0.5 * inv * w * (east[2] - west[2])
                - k * (w - kepler * jnp.sqrt(inv))
                + diffusion * lap[2]
            )

    dust(0, rows // 2)

    for d in range(2):
        for n in range(whole):
            far_copy(d, n).wait_recv()
    for c in order:
        part = slice(c * chunk, (c + 1) * chunk)
        for d, j in ((0, 3), (1, 1)):
            far_copy(d, whole + c).wait_recv()
            total = jnp.dot(near[d, part, :], ga[j], preferred_element_type=F32) + jnp.dot(
                far_in[d, part, :], ga[4 - 4 * d], preferred_element_type=F32
            )
            part_out[d, part, :] = total.astype(BF16)
            part_copy(d, c).start()

    for d in range(2):
        col_out[2, d, 0:1, :] = edge(part_out[d, :, edge_tile(d)].astype(F32), d)
        col_copy(2, d).start()
        col_own[1 - d, 0:1, :] = edge(part_out[d, :, edge_tile(1 - d)].astype(F32), 1 - d)

    load_gr[2].wait()
    middle = jnp.dot(gr[2], ext[...], preferred_element_type=F32).astype(BF16)
    potential[...] = jnp.dot(middle, ga[2], preferred_element_type=F32)
    for d in range(2):
        col_out[1, d, 0:1, :] = edge(potential[:, edge_tile(d)], d)
        col_copy(1, d).start()

    dust(rows // 2, rows)

    for d in range(2):
        col_copy(1, d).wait()
        col_copy(2, d).wait()
        row = col_in[1, d, 0:1, :] + (col_in[2, d, 0:1, :] + col_own[d, 0:1, :])
        dcol[d] = jnp.transpose(jnp.concatenate([row, jnp.zeros((127, rows), F32)], axis=0))

    lanes = lax.broadcasted_iota(jnp.int32, (chunk, arc), 1)
    is_first = lanes == 0
    is_last = lanes == arc - 1
    for c in order:
        part = slice(c * chunk, (c + 1) * chunk)
        for d in range(2):
            part_copy(d, c).wait_recv()
        total = potential[part, :] + (
            part_in[0, part, :].astype(F32) + part_in[1, part, :].astype(F32)
        )
        potential[part, :] = total
        potp[8 + c * chunk : 8 + (c + 1) * chunk, :] = total
        if c == 0:

            @pl.when(has_down)
            def _():
                prow[1].start()

        if c == chunks - 1:

            @pl.when(has_up)
            def _():
                prow[0].start()

        inv = inverse_radius(band * rows + c * chunk, chunk)
        east = jnp.where(is_last, dcol[1, part, 0:1], pltpu.roll(total, arc - 1, 1))
        west = jnp.where(is_first, dcol[0, part, 0:1], pltpu.roll(total, 1, 1))
        azimuth_next[part, :] = azimuth_next[part, :] - 0.5 * gravity * inv * (east - west)

    wait_both(prow)
    for c in order:
        part = slice(c * chunk, (c + 1) * chunk)
        q = potp[c * chunk : (c + 1) * chunk + 16, :]
        radial_next[part, :] = radial_next[part, :] - 0.5 * gravity * (
            q[9 : 9 + chunk] - q[7 : 7 + chunk]
        )
    for d in range(2):
        for n in range(whole + chunks):
            far_copy(d, n).wait_send()
        for c in range(chunks):
            part_copy(d, c).wait_send()


def hand_over(*refs):
    copies = [
        pltpu.make_async_copy(refs[n], refs[4 + n], refs[8].at[n]) for n in range(4)
    ]
    for copy in copies:
        copy.start()
    for copy in copies:
        copy.wait()


def body(gas, green_radial, green_azimuth, rho, u, w, coupling, chunk, strip, pieces):
    rows, arc = rho.shape
    chunks = rows // chunk
    steps = len(pieces)
    dma = pltpu.SemaphoreType.DMA
    operands = (gas, green_radial, green_azimuth, rho, u, w, coupling)
    results = pl.pallas_call(
        functools.partial(kernel, chunk, strip, pieces),
        out_shape=[pltpu.VMEM((rows, arc), F32)] * 4,
        in_specs=[pl.BlockSpec(memory_space=pltpu.HBM)] * 7,
        out_specs=[pl.BlockSpec(memory_space=pltpu.VMEM)] * 4,
        scratch_shapes=[
            pltpu.VMEM((3 * rows, arc), BF16),
            pltpu.VMEM((5, rows, 3 * rows), BF16),
            pltpu.VMEM((5, arc, arc), BF16),
            pltpu.VMEM((3, rows + 16, arc), F32),
            pltpu.VMEM((rows, arc), BF16),
            pltpu.VMEM((rows + 16, arc), F32),
            pltpu.VMEM((2, rows, arc), BF16),
            pltpu.VMEM((2, rows, arc), BF16),
            pltpu.VMEM((2, rows, arc), BF16),
            pltpu.VMEM((2, rows, arc), BF16),
            pltpu.VMEM((2, rows, arc), BF16),
            pltpu.VMEM((3, 2, 8, rows), F32),
            pltpu.VMEM((3, 2, 8, rows), F32),
            pltpu.VMEM((2, 8, rows), F32),
            pltpu.VMEM((2, rows, 128), F32),
            dma((11,)),
            dma((2, steps)),
            dma((2, steps)),
            dma((4,)),
            dma((4,)),
            dma((3, 2)),
            dma((3, 2)),
            dma((2, steps - 1 + chunks)),
            dma((2, steps - 1 + chunks)),
            dma((2, chunks)),
            dma((2, chunks)),
        ],
        compiler_params=pltpu.CompilerParams(
            collective_id=0, has_side_effects=True, vmem_limit_bytes=50 * 2**20
        ),
        name="disc",
    )(*[pltpu.with_memory_space_constraint(x, pltpu.HBM) for x in operands])
    return pl.pallas_call(
        hand_over,
        out_shape=[jax.ShapeDtypeStruct((rows, arc), F32)] * 4,
        in_specs=[pl.BlockSpec(memory_space=pltpu.VMEM)] * 4,
        out_specs=[pl.BlockSpec(memory_space=pl.ANY)] * 4,
        scratch_shapes=[dma((4,))],
        compiler_params=pltpu.CompilerParams(vmem_limit_bytes=2**20),
        name="hand_over",
    )(*[pltpu.with_memory_space_constraint(r, pltpu.VMEM) for r in results])


def solution(mesh, chunk=96, strip=32, pieces=((0, 128), (128, 128), (256, 256))):
    return jax.shard_map(
        functools.partial(body, chunk=chunk, strip=strip, pieces=pieces),
        mesh=mesh,
        in_specs=(
            P("band", "sector"),
            P(None, "band", None),
            P(),
            P("band", "sector"),
            P("band", "sector"),
            P("band", "sector"),
            P("band", "sector"),
        ),
        out_specs=(P("band", "sector"),) * 4,
        check_vma=False,
    )
```

```python
import functools

import jax
import jax.numpy as jnp
from jax import lax
from jax.experimental import pallas as pl
from jax.experimental.pallas import tpu as pltpu
from jax.sharding import PartitionSpec as P

diffusion = 0.1
gravity = 0.1
kepler = 0.6

MESH = pl.DeviceIdType.MESH
F32 = jnp.float32
BF16 = jnp.bfloat16


def kernel(
    chunk,
    strip,
    pieces,
    gas,
    green_radial,
    green_azimuth,
    dust_density,
    dust_radial,
    dust_azimuth,
    coupling,
    potential,
    density_next,
    radial_next,
    azimuth_next,
    ext,
    gr,
    ga,
    fld,
    kv,
    potp,
    near,
    far_out,
    far_in,
    part_out,
    part_in,
    col_out,
    col_in,
    col_own,
    dcol,
    load_sem,
    gas_send,
    gas_recv,
    row_send,
    row_recv,
    col_send,
    col_recv,
    far_send,
    far_recv,
    part_send,
    part_recv,
):
    rows, arc = dust_density.shape
    chunks = rows // chunk
    band = lax.axis_index("band")
    sector = lax.axis_index("sector")
    bands = lax.axis_size("band")
    sectors = lax.axis_size("sector")
    side = (lax.rem(sector + 1, sectors), lax.rem(sector + sectors - 1, sectors))
    side_two = (lax.rem(sector + 2, sectors), lax.rem(sector + sectors - 2, sectors))
    has_up = band < bands - 1
    has_down = band > 0

    def load(src, dst, n):
        copy = pltpu.make_async_copy(src, dst, load_sem.at[n])
        copy.start()
        return copy

    own = pl.ds(rows, rows)
    body_rows = pl.ds(8, rows)
    load_gas = load(gas, ext.at[own, :], 3)
    load_gr = {}
    for n, j in enumerate((4, 0)):
        load_gr[j] = load(green_radial.at[j], gr.at[j], 4 + n)
    load_fields = [
        load(field, fld.at[n, body_rows, :], n)
        for n, field in enumerate((dust_density, dust_radial, dust_azimuth))
    ]
    for n, j in enumerate((3, 1)):
        load_gr[j] = load(green_radial.at[j], gr.at[j], 6 + n)
    load_ga = load(green_azimuth, ga, 9)
    load_gr[2] = load(green_radial.at[2], gr.at[2], 8)
    load_k = load(coupling, kv, 10)

    barrier = pltpu.get_barrier_semaphore()
    for s in side + side_two:
        pl.semaphore_signal(barrier, inc=1, device_id={"sector": s}, device_id_type=MESH)

    @pl.when(has_up)
    def _():
        pl.semaphore_signal(barrier, inc=1, device_id={"band": band + 1}, device_id_type=MESH)

    @pl.when(has_down)
    def _():
        pl.semaphore_signal(barrier, inc=1, device_id={"band": band - 1}, device_id_type=MESH)

    pl.semaphore_wait(barrier, 4 + has_up.astype(jnp.int32) + has_down.astype(jnp.int32))

    def remote(src, dst, send, recv, where):
        return pltpu.make_async_remote_copy(
            src_ref=src,
            dst_ref=dst,
            send_sem=send,
            recv_sem=recv,
            device_id=where,
            device_id_type=MESH,
        )

    up = {"band": band + 1}
    down = {"band": band - 1}

    def gas_copies(n):
        cols = pl.ds(*pieces[n])
        return (
            remote(
                gas.at[:, cols],
                ext.at[pl.ds(0, rows), cols],
                gas_send.at[0, n],
                gas_recv.at[0, n],
                up,
            ),
            remote(
                gas.at[:, cols],
                ext.at[pl.ds(2 * rows, rows), cols],
                gas_send.at[1, n],
                gas_recv.at[1, n],
                down,
            ),
        )

    def start_both(copies):
        @pl.when(has_up)
        def _():
            copies[0].start()

        @pl.when(has_down)
        def _():
            copies[1].start()

    def wait_both(copies):
        @pl.when(has_up)
        def _():
            copies[0].wait_send()
            copies[1].wait_recv()

        @pl.when(has_down)
        def _():
            copies[1].wait_send()
            copies[0].wait_recv()

    for n in range(len(pieces)):
        start_both(gas_copies(n))

    top = pl.ds(rows, 8)
    bottom = pl.ds(8, 8)
    halo_low = pl.ds(0, 8)
    halo_high = pl.ds(rows + 8, 8)
    drow = (
        remote(fld.at[:, top, :], fld.at[:, halo_low, :], row_send.at[0], row_recv.at[0], up),
        remote(fld.at[:, bottom, :], fld.at[:, halo_high, :], row_send.at[1], row_recv.at[1], down),
    )
    prow = (
        remote(potp.at[top, :], potp.at[halo_low, :], row_send.at[2], row_recv.at[2], up),
        remote(potp.at[bottom, :], potp.at[halo_high, :], row_send.at[3], row_recv.at[3], down),
    )

    @pl.when(jnp.logical_not(has_down))
    def _():
        ext[0:rows, :] = jnp.zeros((rows, arc), BF16)
        fld[:, 0:8, :] = jnp.zeros((3, 8, arc), F32)
        potp[0:8, :] = jnp.zeros((8, arc), F32)

    @pl.when(jnp.logical_not(has_up))
    def _():
        ext[2 * rows : 3 * rows, :] = jnp.zeros((rows, arc), BF16)
        fld[:, rows + 8 : rows + 16, :] = jnp.zeros((3, 8, arc), F32)
        potp[rows + 8 : rows + 16, :] = jnp.zeros((8, arc), F32)

    def col_copy(kind, d):
        where = side_two[d] if kind == 2 else side[d]
        return remote(
            col_out.at[kind, d],
            col_in.at[kind, d],
            col_send.at[kind, d],
            col_recv.at[kind, d],
            {"sector": where},
        )

    def edge(tile, d):
        lane = 127 if d == 0 else 0
        return jnp.transpose(tile)[lane : lane + 1, :]

    def edge_tile(d):
        return slice(arc - 128, arc) if d == 0 else slice(0, 128)

    for copy in load_fields:
        copy.wait()
    start_both(drow)
    for d in range(2):
        for n in range(3):
            col_out[0, d, n : n + 1, :] = edge(fld[n, 8 : 8 + rows, edge_tile(d)], d)
        col_copy(0, d).start()

    def far_copy(d, n):
        if n < len(pieces) - 1:
            part, cols = pl.ds(0, rows), pl.ds(*pieces[n])
        else:
            c = n - (len(pieces) - 1)
            part, cols = pl.ds(c * chunk, chunk), pl.ds(*pieces[-1])
        return remote(
            far_out.at[d, part, cols],
            far_in.at[d, part, cols],
            far_send.at[d, n],
            far_recv.at[d, n],
            {"sector": side[d]},
        )

    rim = 16

    def span(c):
        if c >= chunks:
            return (0, rim) if c == chunks else (rows - rim, rim)
        low = c * chunk + (rim if c == 0 else 0)
        return low, (c + 1) * chunk - (rim if c == chunks - 1 else 0) - low

    def part_copy(d, c):
        part = pl.ds(*span(c))
        return remote(
            part_out.at[d, part, :],
            part_in.at[d, part, :],
            part_send.at[d, c],
            part_recv.at[d, c],
            {"sector": side[d]},
        )

    order = [(chunks - n) % chunks for n in range(chunks)]
    whole = len(pieces) - 1
    load_gas.wait()
    load_gr[4].wait()
    load_gr[0].wait()
    for n in range(whole):
        wait_both(gas_copies(n))
        cols = slice(pieces[n][0], pieces[n][0] + pieces[n][1])
        for d, j in ((0, 4), (1, 0)):
            far_out[d, :, cols] = jnp.dot(
                gr[j], ext[:, cols], preferred_element_type=F32
            ).astype(BF16)
            far_copy(d, n).start()
    wait_both(gas_copies(whole))
    last = slice(pieces[-1][0], arc)
    for c in order:
        part = slice(c * chunk, (c + 1) * chunk)
        for d, j in ((0, 4), (1, 0)):
            far_out[d, part, last] = jnp.dot(
                gr[j, part, :], ext[:, last], preferred_element_type=F32
            ).astype(BF16)
            far_copy(d, whole + c).start()

    load_gr[3].wait()
    load_gr[1].wait()
    load_ga.wait()
    for d, j in ((0, 3), (1, 1)):
        near[d] = jnp.dot(gr[j], ext[...], preferred_element_type=F32).astype(BF16)

    load_k.wait()
    for d in range(2):
        col_copy(0, d).wait()
    wait_both(drow)

    def columns(block):
        return jnp.transpose(jnp.concatenate([block, jnp.zeros((120, rows), F32)], axis=0))

    for d in range(2):
        dcol[d] = columns(col_in[0, d])

    total_rows = rows * bands

    def inverse_radius(first, count):
        index = first + lax.broadcasted_iota(jnp.int32, (count, 1), 0)
        return 1.0 / (1.0 + 3.0 * (index.astype(F32) + 0.5) / total_rows)

    def dust(start, stop):
        lanes = lax.broadcasted_iota(jnp.int32, (strip, arc), 1)
        is_first = lanes == 0
        is_last = lanes == arc - 1

        @pl.loop(start // strip, stop // strip)
        def _(step):
            first = pl.multiple_of(step * strip, strip)
            part = pl.ds(first, strip)
            window = pl.ds(first, strip + 16)
            inv = inverse_radius(band * rows + first, strip)
            west_edge = dcol[0, part, :]
            east_edge = dcol[1, part, :]
            centre, above, below, east, west = [], [], [], [], []
            for n in range(3):
                q = fld[n, window, :]
                mid = q[8 : 8 + strip]
                centre.append(mid)
                above.append(q[9 : 9 + strip])
                below.append(q[7 : 7 + strip])
                east.append(
                    jnp.where(is_last, east_edge[:, n : n + 1], pltpu.roll(mid, arc - 1, 1))
                )
                west.append(jnp.where(is_first, west_edge[:, n : n + 1], pltpu.roll(mid, 1, 1)))
            rho, u, w = centre
            k = kv[part, :].astype(F32)
            lap = [above[n] + below[n] + east[n] + west[n] - 4.0 * centre[n] for n in range(3)]
            density_next[part, :] = (
                rho
                - 0.5 * (above[0] * above[1] - below[0] * below[1])
                - 0.5 * inv * (east[0] * east[2] - west[0] * west[2])
                + diffusion * lap[0]
            )
            radial_next[part, :] = (
                u
                - 0.5 * u * (above[1] - below[1])
                - 0.5 * inv * w * (east[1] - west[1])
                - k * u
                + diffusion * lap[1]
            )
            azimuth_next[part, :] = (
                w
                - 0.5 * u * (above[2] - below[2])
                - 0.5 * inv * w * (east[2] - west[2])
                - k * (w - kepler * jnp.sqrt(inv))
                + diffusion * lap[2]
            )

    dust(0, rows // 2)

    for d in range(2):
        for n in range(whole):
            far_copy(d, n).wait_recv()
    def both_rims(block):
        return jnp.concatenate([block[0:rim, :], block[rows - rim : rows, :]], axis=0)

    for d, j in ((0, 3), (1, 1)):
        far_copy(d, whole).wait_recv()
        far_copy(d, whole + chunks - 1).wait_recv()
        total = (
            jnp.dot(both_rims(near.at[d]), ga[j], preferred_element_type=F32)
            + jnp.dot(both_rims(far_in.at[d]), ga[4 - 4 * d], preferred_element_type=F32)
        ).astype(BF16)
        part_out[d, 0:rim, :] = total[0:rim]
        part_out[d, rows - rim : rows, :] = total[rim:]
        part_copy(d, chunks).start()
        part_copy(d, chunks + 1).start()
    for c in order:
        low, count = span(c)
        part = slice(low, low + count)
        for d, j in ((0, 3), (1, 1)):
            if c not in (0, chunks - 1):
                far_copy(d, whole + c).wait_recv()
            total = jnp.dot(near[d, part, :], ga[j], preferred_element_type=F32) + jnp.dot(
                far_in[d, part, :], ga[4 - 4 * d], preferred_element_type=F32
            )
            part_out[d, part, :] = total.astype(BF16)
            part_copy(d, c).start()

    for d in range(2):
        col_out[2, d, 0:1, :] = edge(part_out[d, :, edge_tile(d)].astype(F32), d)
        col_copy(2, d).start()
        col_own[1 - d, 0:1, :] = edge(part_out[d, :, edge_tile(1 - d)].astype(F32), 1 - d)

    load_gr[2].wait()
    middle = jnp.dot(gr[2], ext[...], preferred_element_type=F32).astype(BF16)
    potential[...] = jnp.dot(middle, ga[2], preferred_element_type=F32)
    for d in range(2):
        col_out[1, d, 0:1, :] = edge(potential[:, edge_tile(d)], d)
        col_copy(1, d).start()

    def settle(low, count):
        part = slice(low, low + count)
        total = potential[part, :] + (
            part_in[0, part, :].astype(F32) + part_in[1, part, :].astype(F32)
        )
        potential[part, :] = total
        potp[8 + low : 8 + low + count, :] = total
        return total

    for d in range(2):
        part_copy(d, chunks).wait_recv()
        part_copy(d, chunks + 1).wait_recv()
    settle(0, rim)
    settle(rows - rim, rim)
    start_both(prow)

    dust(rows // 2, rows)

    for d in range(2):
        col_copy(1, d).wait()
        col_copy(2, d).wait()
        row = col_in[1, d, 0:1, :] + (col_in[2, d, 0:1, :] + col_own[d, 0:1, :])
        dcol[d] = jnp.transpose(jnp.concatenate([row, jnp.zeros((127, rows), F32)], axis=0))

    lanes = lax.broadcasted_iota(jnp.int32, (chunk, arc), 1)
    is_first = lanes == 0
    is_last = lanes == arc - 1
    for c in order:
        part = slice(c * chunk, (c + 1) * chunk)
        for d in range(2):
            part_copy(d, c).wait_recv()
        settle(*span(c))
        total = potential[part, :]
        inv = inverse_radius(band * rows + c * chunk, chunk)
        east = jnp.where(is_last, dcol[1, part, 0:1], pltpu.roll(total, arc - 1, 1))
        west = jnp.where(is_first, dcol[0, part, 0:1], pltpu.roll(total, 1, 1))
        azimuth_next[part, :] = azimuth_next[part, :] - 0.5 * gravity * inv * (east - west)

    wait_both(prow)
    for c in order:
        part = slice(c * chunk, (c + 1) * chunk)
        q = potp[c * chunk : (c + 1) * chunk + 16, :]
        radial_next[part, :] = radial_next[part, :] - 0.5 * gravity * (
            q[9 : 9 + chunk] - q[7 : 7 + chunk]
        )
    for d in range(2):
        for n in range(whole + chunks):
            far_copy(d, n).wait_send()
        for c in range(chunks + 2):
            part_copy(d, c).wait_send()


def hand_over(*refs):
    copies = [
        pltpu.make_async_copy(refs[n], refs[4 + n], refs[8].at[n]) for n in range(4)
    ]
    for copy in copies:
        copy.start()
    for copy in copies:
        copy.wait()


def body(gas, green_radial, green_azimuth, rho, u, w, coupling, chunk, strip, pieces):
    rows, arc = rho.shape
    chunks = rows // chunk
    steps = len(pieces)
    dma = pltpu.SemaphoreType.DMA
    operands = (gas, green_radial, green_azimuth, rho, u, w, coupling)
    results = pl.pallas_call(
        functools.partial(kernel, chunk, strip, pieces),
        out_shape=[pltpu.VMEM((rows, arc), F32)] * 4,
        in_specs=[pl.BlockSpec(memory_space=pltpu.HBM)] * 7,
        out_specs=[pl.BlockSpec(memory_space=pltpu.VMEM)] * 4,
        scratch_shapes=[
            pltpu.VMEM((3 * rows, arc), BF16),
            pltpu.VMEM((5, rows, 3 * rows), BF16),
            pltpu.VMEM((5, arc, arc), BF16),
            pltpu.VMEM((3, rows + 16, arc), F32),
            pltpu.VMEM((rows, arc), BF16),
            pltpu.VMEM((rows + 16, arc), F32),
            pltpu.VMEM((2, rows, arc), BF16),
            pltpu.VMEM((2, rows, arc), BF16),
            pltpu.VMEM((2, rows, arc), BF16),
            pltpu.VMEM((2, rows, arc), BF16),
            pltpu.VMEM((2, rows, arc), BF16),
            pltpu.VMEM((3, 2, 8, rows), F32),
            pltpu.VMEM((3, 2, 8, rows), F32),
            pltpu.VMEM((2, 8, rows), F32),
            pltpu.VMEM((2, rows, 128), F32),
            dma((11,)),
            dma((2, steps)),
            dma((2, steps)),
            dma((4,)),
            dma((4,)),
            dma((3, 2)),
            dma((3, 2)),
            dma((2, steps - 1 + chunks)),
            dma((2, steps - 1 + chunks)),
            dma((2, chunks + 2)),
            dma((2, chunks + 2)),
        ],
        compiler_params=pltpu.CompilerParams(
            collective_id=0, has_side_effects=True, vmem_limit_bytes=50 * 2**20
        ),
        name="disc",
    )(*[pltpu.with_memory_space_constraint(x, pltpu.HBM) for x in operands])
    return pl.pallas_call(
        hand_over,
        out_shape=[jax.ShapeDtypeStruct((rows, arc), F32)] * 4,
        in_specs=[pl.BlockSpec(memory_space=pltpu.VMEM)] * 4,
        out_specs=[pl.BlockSpec(memory_space=pl.ANY)] * 4,
        scratch_shapes=[dma((4,))],
        compiler_params=pltpu.CompilerParams(vmem_limit_bytes=2**20),
        name="hand_over",
    )(*[pltpu.with_memory_space_constraint(r, pltpu.VMEM) for r in results])


def solution(mesh, chunk=96, strip=32, pieces=((0, 128), (128, 128), (256, 256))):
    return jax.shard_map(
        functools.partial(body, chunk=chunk, strip=strip, pieces=pieces),
        mesh=mesh,
        in_specs=(
            P("band", "sector"),
            P(None, "band", None),
            P(),
            P("band", "sector"),
            P("band", "sector"),
            P("band", "sector"),
            P("band", "sector"),
        ),
        out_specs=(P("band", "sector"),) * 4,
        check_vma=False,
    )
```

```python
import functools

import jax
import jax.numpy as jnp
from jax import lax
from jax.experimental import pallas as pl
from jax.experimental.pallas import tpu as pltpu
from jax.sharding import PartitionSpec as P

diffusion = 0.1
gravity = 0.1
kepler = 0.6

MESH = pl.DeviceIdType.MESH
F32 = jnp.float32
BF16 = jnp.bfloat16


def kernel(
    chunk,
    strip,
    pieces,
    gas,
    green_radial,
    green_azimuth,
    dust_density,
    dust_radial,
    dust_azimuth,
    coupling,
    potential,
    density_next,
    radial_next,
    azimuth_next,
    ext,
    gz,
    gr,
    ga,
    fld,
    kv,
    potp,
    near,
    far_out,
    far_in,
    part_out,
    part_in,
    col_out,
    col_in,
    col_own,
    dcol,
    load_sem,
    gas_send,
    gas_recv,
    first_send,
    first_recv,
    row_send,
    row_recv,
    col_send,
    col_recv,
    far_send,
    far_recv,
    part_send,
    part_recv,
):
    rows, arc = dust_density.shape
    chunks = rows // chunk
    band = lax.axis_index("band")
    sector = lax.axis_index("sector")
    bands = lax.axis_size("band")
    sectors = lax.axis_size("sector")
    side = (lax.rem(sector + 1, sectors), lax.rem(sector + sectors - 1, sectors))
    side_two = (lax.rem(sector + 2, sectors), lax.rem(sector + sectors - 2, sectors))
    has_up = band < bands - 1
    has_down = band > 0
    seam_up = band == bands // 2 - 1
    seam_down = band == bands // 2

    lead = gz.shape[2]
    whole = len(pieces) - 2

    def load(src, dst, n):
        copy = pltpu.make_async_copy(src, dst, load_sem.at[n])
        copy.start()
        return copy

    own = pl.ds(rows, rows)
    body_rows = pl.ds(8, rows)
    load_gas = load(gas, ext.at[own, :], 3)
    load_gr = {}
    for n, j in enumerate((4, 0)):
        load_gr[j] = load(green_radial.at[j], gr.at[j], 4 + n)
    load_fields = [
        load(field, fld.at[n, body_rows, :], n)
        for n, field in enumerate((dust_density, dust_radial, dust_azimuth))
    ]
    for n, j in enumerate((3, 1)):
        load_gr[j] = load(green_radial.at[j], gr.at[j], 6 + n)
    load_ga = load(green_azimuth, ga, 9)
    load_gr[2] = load(green_radial.at[2], gr.at[2], 8)
    load_k = load(coupling, kv, 10)

    barrier = pltpu.get_barrier_semaphore()
    for s in side + side_two:
        pl.semaphore_signal(barrier, inc=1, device_id={"sector": s}, device_id_type=MESH)

    @pl.when(has_up)
    def _():
        pl.semaphore_signal(barrier, inc=1, device_id={"band": band + 1}, device_id_type=MESH)

    @pl.when(has_down)
    def _():
        pl.semaphore_signal(barrier, inc=1, device_id={"band": band - 1}, device_id_type=MESH)

    pl.semaphore_wait(barrier, 4 + has_up.astype(jnp.int32) + has_down.astype(jnp.int32))

    def remote(src, dst, send, recv, where):
        return pltpu.make_async_remote_copy(
            src_ref=src,
            dst_ref=dst,
            send_sem=send,
            recv_sem=recv,
            device_id=where,
            device_id_type=MESH,
        )

    up = {"band": band + 1}
    down = {"band": band - 1}

    def gas_copies(n):
        cols = pl.ds(*pieces[n])
        return (
            remote(
                gas.at[:, cols],
                ext.at[pl.ds(0, rows), cols],
                gas_send.at[0, n],
                gas_recv.at[0, n],
                up,
            ),
            remote(
                gas.at[:, cols],
                ext.at[pl.ds(2 * rows, rows), cols],
                gas_send.at[1, n],
                gas_recv.at[1, n],
                down,
            ),
        )

    def start_both(copies):
        @pl.when(has_up)
        def _():
            copies[0].start()

        @pl.when(has_down)
        def _():
            copies[1].start()

    def wait_both(copies):
        @pl.when(has_up)
        def _():
            copies[0].wait_send()
            copies[1].wait_recv()

        @pl.when(has_down)
        def _():
            copies[1].wait_send()
            copies[0].wait_recv()

    thirds = [pl.ds(n * rows, rows) for n in range(3)]

    def first_copy(d, third, src, where, sent):
        return remote(
            src, gz.at[d, thirds[third], :], first_send.at[d, sent], first_recv.at[d, third], where
        )

    head = pl.ds(0, lead)

    def first_own(d):
        return first_copy(d, 1, gas.at[:, head], {"sector": side[d]}, 1)

    def first_on(d, third):
        where = up if third == 0 else down
        return first_copy(d, third, gz.at[d, thirds[1], :], where, third)

    def first_seam(d, third):
        return first_copy(d, third, ext.at[thirds[third], head], {"sector": side[d]}, 2 - third)

    for d in range(2):
        first_own(d).start()
    def on_seam(up_step, down_step):
        pl.when(seam_up)(up_step)
        pl.when(seam_down)(down_step)

    def off_seam(up_step, down_step):
        pl.when(jnp.logical_and(has_up, jnp.logical_not(seam_up)))(up_step)
        pl.when(jnp.logical_and(has_down, jnp.logical_not(seam_down)))(down_step)

    def arrive(copies):
        def from_up():
            copies[0].wait_send()
            copies[1].wait_recv()

        def from_down():
            copies[1].wait_send()
            copies[0].wait_recv()

        return from_up, from_down

    def leave(copies):
        return copies[0].start, copies[1].start

    on_seam(*leave(gas_copies(whole + 1)))
    for n in range(whole + 1):
        start_both(gas_copies(n))
    off_seam(*leave(gas_copies(whole + 1)))

    top = pl.ds(rows, 8)
    bottom = pl.ds(8, 8)
    halo_low = pl.ds(0, 8)
    halo_high = pl.ds(rows + 8, 8)
    drow = (
        remote(fld.at[:, top, :], fld.at[:, halo_low, :], row_send.at[0], row_recv.at[0], up),
        remote(fld.at[:, bottom, :], fld.at[:, halo_high, :], row_send.at[1], row_recv.at[1], down),
    )
    prow = (
        remote(potp.at[top, :], potp.at[halo_low, :], row_send.at[2], row_recv.at[2], up),
        remote(potp.at[bottom, :], potp.at[halo_high, :], row_send.at[3], row_recv.at[3], down),
    )

    @pl.when(jnp.logical_not(has_down))
    def _():
        ext[0:rows, :] = jnp.zeros((rows, arc), BF16)
        gz[:, 0:rows, :] = jnp.zeros((2, rows, lead), BF16)
        fld[:, 0:8, :] = jnp.zeros((3, 8, arc), F32)
        potp[0:8, :] = jnp.zeros((8, arc), F32)

    @pl.when(jnp.logical_not(has_up))
    def _():
        ext[2 * rows : 3 * rows, :] = jnp.zeros((rows, arc), BF16)
        gz[:, 2 * rows : 3 * rows, :] = jnp.zeros((2, rows, lead), BF16)
        fld[:, rows + 8 : rows + 16, :] = jnp.zeros((3, 8, arc), F32)
        potp[rows + 8 : rows + 16, :] = jnp.zeros((8, arc), F32)

    def col_copy(kind, d):
        where = side_two[d] if kind == 2 else side[d]
        return remote(
            col_out.at[kind, d],
            col_in.at[kind, d],
            col_send.at[kind, d],
            col_recv.at[kind, d],
            {"sector": where},
        )

    def edge(tile, d):
        lane = 127 if d == 0 else 0
        return jnp.transpose(tile)[lane : lane + 1, :]

    def edge_tile(d):
        return slice(arc - 128, arc) if d == 0 else slice(0, 128)

    for copy in load_fields:
        copy.wait()
    start_both(drow)
    for d in range(2):
        for n in range(3):
            col_out[0, d, n : n + 1, :] = edge(fld[n, 8 : 8 + rows, edge_tile(d)], d)
        col_copy(0, d).start()

    def far_copy(d, n):
        if n < whole:
            part, cols = pl.ds(0, rows), pl.ds(*pieces[n])
        else:
            part, cols = pl.ds((n - whole) * chunk, chunk), pl.ds(*pieces[whole])
        return remote(
            far_out.at[d, part, cols],
            far_in.at[d, part, cols],
            far_send.at[d, n],
            far_recv.at[d, n],
            {"sector": side[d]},
        )

    rim = 16

    def span(c):
        if c >= chunks:
            return (0, rim) if c == chunks else (rows - rim, rim)
        low = c * chunk + (rim if c == 0 else 0)
        return low, (c + 1) * chunk - (rim if c == chunks - 1 else 0) - low

    def part_copy(d, c):
        part = pl.ds(*span(c))
        return remote(
            part_out.at[d, part, :],
            part_in.at[d, part, :],
            part_send.at[d, c],
            part_recv.at[d, c],
            {"sector": side[d]},
        )

    order = [(chunks - n) % chunks for n in range(chunks)]
    load_gas.wait()
    load_gr[4].wait()
    load_gr[0].wait()
    def pass_on():
        for d in range(2):
            first_own(d).wait()
            off_seam(first_on(d, 0).start, first_on(d, 2).start)

    early = jnp.logical_or(lax.rem(band, 2) == 1, seam_down)
    pl.when(early)(pass_on)
    on_seam(*arrive(gas_copies(whole + 1)))
    for d in range(2):
        on_seam(first_seam(d, 2).start, first_seam(d, 0).start)

    for n in range(whole):
        wait_both(gas_copies(n))
        cols = slice(pieces[n][0], pieces[n][0] + pieces[n][1])
        for d, j in ((0, 4), (1, 0)):
            far_out[d, :, cols] = jnp.dot(
                gr[j], ext[:, cols], preferred_element_type=F32
            ).astype(BF16)
            far_copy(d, n).start()
    pl.when(jnp.logical_not(early))(pass_on)
    wait_both(gas_copies(whole))
    last = slice(pieces[whole][0], pieces[whole][0] + pieces[whole][1])
    for c in order:
        part = slice(c * chunk, (c + 1) * chunk)
        for d, j in ((0, 4), (1, 0)):
            far_out[d, part, last] = jnp.dot(
                gr[j, part, :], ext[:, last], preferred_element_type=F32
            ).astype(BF16)
            far_copy(d, whole + c).start()

    off_seam(*arrive(gas_copies(whole + 1)))
    load_gr[3].wait()
    load_gr[1].wait()
    load_ga.wait()
    for d, j in ((0, 3), (1, 1)):
        near[d] = jnp.dot(gr[j], ext[...], preferred_element_type=F32).astype(BF16)

    for d, j in ((0, 4), (1, 0)):

        @pl.when(has_up)
        def _():
            first_on(d, 0).wait_send()
            first_on(d, 2).wait_recv()

        @pl.when(has_down)
        def _():
            first_on(d, 2).wait_send()
            first_on(d, 0).wait_recv()

        far_in[d, :, 0:lead] = jnp.dot(gr[j], gz[d], preferred_element_type=F32).astype(BF16)
    for d in range(2):
        for n in range(whole):
            far_copy(d, n).wait_recv()
    for c in order:
        part = slice(c * chunk, (c + 1) * chunk)
        for d, j in ((0, 3), (1, 1)):
            far_copy(d, whole + c).wait_recv()
            total = jnp.dot(near[d, part, :], ga[j], preferred_element_type=F32) + jnp.dot(
                far_in[d, part, :], ga[4 - 4 * d], preferred_element_type=F32
            )
            part_out[d, part, :] = total.astype(BF16)
            if c == 0:
                part_copy(d, chunks).start()
            if c == chunks - 1:
                part_copy(d, chunks + 1).start()
            part_copy(d, c).start()

    for d in range(2):
        col_out[2, d, 0:1, :] = edge(part_out[d, :, edge_tile(d)].astype(F32), d)
        col_copy(2, d).start()
        col_own[1 - d, 0:1, :] = edge(part_out[d, :, edge_tile(1 - d)].astype(F32), 1 - d)

    load_gr[2].wait()
    middle = jnp.dot(gr[2], ext[...], preferred_element_type=F32).astype(BF16)
    potential[...] = jnp.dot(middle, ga[2], preferred_element_type=F32)
    for d in range(2):
        col_out[1, d, 0:1, :] = edge(potential[:, edge_tile(d)], d)
        col_copy(1, d).start()

    load_k.wait()
    for d in range(2):
        col_copy(0, d).wait()
    wait_both(drow)

    def columns(block):
        return jnp.transpose(jnp.concatenate([block, jnp.zeros((120, rows), F32)], axis=0))

    for d in range(2):
        dcol[d] = columns(col_in[0, d])

    total_rows = rows * bands

    def inverse_radius(first, count):
        index = first + lax.broadcasted_iota(jnp.int32, (count, 1), 0)
        return 1.0 / (1.0 + 3.0 * (index.astype(F32) + 0.5) / total_rows)

    def dust(start, stop):
        lanes = lax.broadcasted_iota(jnp.int32, (strip, arc), 1)
        is_first = lanes == 0
        is_last = lanes == arc - 1

        @pl.loop(start // strip, stop // strip)
        def _(step):
            first = pl.multiple_of(step * strip, strip)
            part = pl.ds(first, strip)
            window = pl.ds(first, strip + 16)
            inv = inverse_radius(band * rows + first, strip)
            west_edge = dcol[0, part, :]
            east_edge = dcol[1, part, :]
            centre, above, below, east, west = [], [], [], [], []
            for n in range(3):
                q = fld[n, window, :]
                mid = q[8 : 8 + strip]
                centre.append(mid)
                above.append(q[9 : 9 + strip])
                below.append(q[7 : 7 + strip])
                east.append(
                    jnp.where(is_last, east_edge[:, n : n + 1], pltpu.roll(mid, arc - 1, 1))
                )
                west.append(jnp.where(is_first, west_edge[:, n : n + 1], pltpu.roll(mid, 1, 1)))
            rho, u, w = centre
            k = kv[part, :].astype(F32)
            lap = [above[n] + below[n] + east[n] + west[n] - 4.0 * centre[n] for n in range(3)]
            density_next[part, :] = (
                rho
                - 0.5 * (above[0] * above[1] - below[0] * below[1])
                - 0.5 * inv * (east[0] * east[2] - west[0] * west[2])
                + diffusion * lap[0]
            )
            radial_next[part, :] = (
                u
                - 0.5 * u * (above[1] - below[1])
                - 0.5 * inv * w * (east[1] - west[1])
                - k * u
                + diffusion * lap[1]
            )
            azimuth_next[part, :] = (
                w
                - 0.5 * u * (above[2] - below[2])
                - 0.5 * inv * w * (east[2] - west[2])
                - k * (w - kepler * jnp.sqrt(inv))
                + diffusion * lap[2]
            )

    def settle(low, count):
        part = slice(low, low + count)
        total = potential[part, :] + (
            part_in[0, part, :].astype(F32) + part_in[1, part, :].astype(F32)
        )
        potential[part, :] = total
        potp[8 + low : 8 + low + count, :] = total
        return total

    for d in range(2):
        part_copy(d, chunks).wait_recv()
        part_copy(d, chunks + 1).wait_recv()
    settle(0, rim)
    settle(rows - rim, rim)
    start_both(prow)

    dust(0, rows)

    for d in range(2):
        col_copy(1, d).wait()
        col_copy(2, d).wait()
        row = col_in[1, d, 0:1, :] + (col_in[2, d, 0:1, :] + col_own[d, 0:1, :])
        dcol[d] = jnp.transpose(jnp.concatenate([row, jnp.zeros((127, rows), F32)], axis=0))

    lanes = lax.broadcasted_iota(jnp.int32, (chunk, arc), 1)
    is_first = lanes == 0
    is_last = lanes == arc - 1
    for c in order:
        part = slice(c * chunk, (c + 1) * chunk)
        for d in range(2):
            part_copy(d, c).wait_recv()
        settle(*span(c))
        total = potential[part, :]
        inv = inverse_radius(band * rows + c * chunk, chunk)
        east = jnp.where(is_last, dcol[1, part, 0:1], pltpu.roll(total, arc - 1, 1))
        west = jnp.where(is_first, dcol[0, part, 0:1], pltpu.roll(total, 1, 1))
        azimuth_next[part, :] = azimuth_next[part, :] - 0.5 * gravity * inv * (east - west)

    wait_both(prow)
    for c in order:
        part = slice(c * chunk, (c + 1) * chunk)
        q = potp[c * chunk : (c + 1) * chunk + 16, :]
        radial_next[part, :] = radial_next[part, :] - 0.5 * gravity * (
            q[9 : 9 + chunk] - q[7 : 7 + chunk]
        )
    for d in range(2):
        for n in range(whole + chunks):
            far_copy(d, n).wait_send()
        for c in range(chunks + 2):
            part_copy(d, c).wait_send()


def hand_over(*refs):
    copies = [
        pltpu.make_async_copy(refs[n], refs[4 + n], refs[8].at[n]) for n in range(4)
    ]
    for copy in copies:
        copy.start()
    for copy in copies:
        copy.wait()


def body(gas, green_radial, green_azimuth, rho, u, w, coupling, chunk, strip, pieces):
    lead = pieces[-1][1]
    rows, arc = rho.shape
    chunks = rows // chunk
    steps = len(pieces)
    dma = pltpu.SemaphoreType.DMA
    operands = (gas, green_radial, green_azimuth, rho, u, w, coupling)
    results = pl.pallas_call(
        functools.partial(kernel, chunk, strip, pieces),
        out_shape=[pltpu.VMEM((rows, arc), F32)] * 4,
        in_specs=[pl.BlockSpec(memory_space=pltpu.HBM)] * 7,
        out_specs=[pl.BlockSpec(memory_space=pltpu.VMEM)] * 4,
        scratch_shapes=[
            pltpu.VMEM((3 * rows, arc), BF16),
            pltpu.VMEM((2, 3 * rows, lead), BF16),
            pltpu.VMEM((5, rows, 3 * rows), BF16),
            pltpu.VMEM((5, arc, arc), BF16),
            pltpu.VMEM((3, rows + 16, arc), F32),
            pltpu.VMEM((rows, arc), BF16),
            pltpu.VMEM((rows + 16, arc), F32),
            pltpu.VMEM((2, rows, arc), BF16),
            pltpu.VMEM((2, rows, arc), BF16),
            pltpu.VMEM((2, rows, arc), BF16),
            pltpu.VMEM((2, rows, arc), BF16),
            pltpu.VMEM((2, rows, arc), BF16),
            pltpu.VMEM((3, 2, 8, rows), F32),
            pltpu.VMEM((3, 2, 8, rows), F32),
            pltpu.VMEM((2, 8, rows), F32),
            pltpu.VMEM((2, rows, 128), F32),
            dma((11,)),
            dma((2, steps)),
            dma((2, steps)),
            dma((2, 3)),
            dma((2, 3)),
            dma((4,)),
            dma((4,)),
            dma((3, 2)),
            dma((3, 2)),
            dma((2, steps - 2 + chunks)),
            dma((2, steps - 2 + chunks)),
            dma((2, chunks + 2)),
            dma((2, chunks + 2)),
        ],
        compiler_params=pltpu.CompilerParams(
            collective_id=0, has_side_effects=True, vmem_limit_bytes=50 * 2**20
        ),
        name="disc",
    )(*[pltpu.with_memory_space_constraint(x, pltpu.HBM) for x in operands])
    return pl.pallas_call(
        hand_over,
        out_shape=[jax.ShapeDtypeStruct((rows, arc), F32)] * 4,
        in_specs=[pl.BlockSpec(memory_space=pltpu.VMEM)] * 4,
        out_specs=[pl.BlockSpec(memory_space=pl.ANY)] * 4,
        scratch_shapes=[dma((4,))],
        compiler_params=pltpu.CompilerParams(vmem_limit_bytes=2**20),
        name="hand_over",
    )(*[pltpu.with_memory_space_constraint(r, pltpu.VMEM) for r in results])


def solution(mesh, chunk=96, strip=32, pieces=((128, 128), (256, 256), (0, 128))):
    return jax.shard_map(
        functools.partial(body, chunk=chunk, strip=strip, pieces=pieces),
        mesh=mesh,
        in_specs=(
            P("band", "sector"),
            P(None, "band", None),
            P(),
            P("band", "sector"),
            P("band", "sector"),
            P("band", "sector"),
            P("band", "sector"),
        ),
        out_specs=(P("band", "sector"),) * 4,
        check_vma=False,
    )
```

```python
import functools

import jax
import jax.numpy as jnp
from jax import lax
from jax.experimental import pallas as pl
from jax.experimental.pallas import tpu as pltpu
from jax.sharding import PartitionSpec as P

diffusion = 0.1
gravity = 0.1
kepler = 0.6

MESH = pl.DeviceIdType.MESH
F32 = jnp.float32
BF16 = jnp.bfloat16


def inverse_radius(first, count, total_rows):
    index = first + lax.broadcasted_iota(jnp.int32, (count, 1), 0)
    return 1.0 / (1.0 + 3.0 * (index.astype(F32) + 0.5) / total_rows)


def kernel(
    chunk,
    strip,
    pieces,
    gas,
    green_radial,
    green_azimuth,
    dust_density,
    dust_radial,
    dust_azimuth,
    coupling,
    potp,
    edges,
    density_next,
    radial_next,
    azimuth_next,
    ext,
    gz,
    gr,
    ga,
    fld,
    kv,
    prow_in,
    near,
    far_out,
    far_in,
    part_out,
    part_in,
    col_out,
    col_in,
    col_own,
    dcol,
    load_sem,
    gas_send,
    gas_recv,
    first_send,
    first_recv,
    row_send,
    row_recv,
    col_send,
    col_recv,
    far_send,
    far_recv,
    part_send,
    part_recv,
):
    rows, arc = dust_density.shape
    chunks = rows // chunk
    band = lax.axis_index("band")
    sector = lax.axis_index("sector")
    bands = lax.axis_size("band")
    sectors = lax.axis_size("sector")
    side = (lax.rem(sector + 1, sectors), lax.rem(sector + sectors - 1, sectors))
    side_two = (lax.rem(sector + 2, sectors), lax.rem(sector + sectors - 2, sectors))
    has_up = band < bands - 1
    has_down = band > 0
    seam_up = band == bands // 2 - 1
    seam_down = band == bands // 2

    lead = gz.shape[2]
    whole = len(pieces) - 2

    def load(src, dst, n):
        copy = pltpu.make_async_copy(src, dst, load_sem.at[n])
        copy.start()
        return copy

    own = pl.ds(rows, rows)
    body_rows = pl.ds(8, rows)
    load_gas = load(gas, ext.at[own, :], 3)
    load_gr = {}
    for n, j in enumerate((4, 0)):
        load_gr[j] = load(green_radial.at[j], gr.at[j], 4 + n)
    load_fields = [
        load(field, fld.at[n, body_rows, :], n)
        for n, field in enumerate((dust_density, dust_radial, dust_azimuth))
    ]
    load_inner = load(green_radial.at[pl.ds(1, 3)], gr.at[pl.ds(1, 3)], 6)
    load_ga = load(green_azimuth, ga, 7)
    load_k = load(coupling, kv, 8)

    barrier = pltpu.get_barrier_semaphore()
    for s in side + side_two:
        pl.semaphore_signal(barrier, inc=1, device_id={"sector": s}, device_id_type=MESH)

    @pl.when(has_up)
    def _():
        pl.semaphore_signal(barrier, inc=1, device_id={"band": band + 1}, device_id_type=MESH)

    @pl.when(has_down)
    def _():
        pl.semaphore_signal(barrier, inc=1, device_id={"band": band - 1}, device_id_type=MESH)

    pl.semaphore_wait(barrier, 4 + has_up.astype(jnp.int32) + has_down.astype(jnp.int32))

    def remote(src, dst, send, recv, where):
        return pltpu.make_async_remote_copy(
            src_ref=src,
            dst_ref=dst,
            send_sem=send,
            recv_sem=recv,
            device_id=where,
            device_id_type=MESH,
        )

    up = {"band": band + 1}
    down = {"band": band - 1}

    def gas_copies(n):
        cols = pl.ds(*pieces[n])
        return (
            remote(
                gas.at[:, cols],
                ext.at[pl.ds(0, rows), cols],
                gas_send.at[0],
                gas_recv.at[0, n],
                up,
            ),
            remote(
                gas.at[:, cols],
                ext.at[pl.ds(2 * rows, rows), cols],
                gas_send.at[1],
                gas_recv.at[1, n],
                down,
            ),
        )

    def both(up_step, down_step):
        pl.when(has_up)(up_step)
        pl.when(has_down)(down_step)

    def start_both(copies):
        both(copies[0].start, copies[1].start)

    def wait_both(copies):
        @pl.when(has_up)
        def _():
            copies[0].wait_send()
            copies[1].wait_recv()

        @pl.when(has_down)
        def _():
            copies[1].wait_send()
            copies[0].wait_recv()

    thirds = [pl.ds(n * rows, rows) for n in range(3)]

    def first_copy(d, third, src, where, sent):
        return remote(
            src, gz.at[d, thirds[third], :], first_send.at[d, sent], first_recv.at[d, third], where
        )

    head = pl.ds(0, lead)

    def first_own(d):
        return first_copy(d, 1, gas.at[:, head], {"sector": side[d]}, 1)

    def first_on(d, third):
        where = up if third == 0 else down
        return first_copy(d, third, gz.at[d, thirds[1], :], where, third)

    def first_seam(d, third):
        return first_copy(d, third, ext.at[thirds[third], head], {"sector": side[d]}, 2 - third)

    for d in range(2):
        first_own(d).start()
    def on_seam(up_step, down_step):
        pl.when(seam_up)(up_step)
        pl.when(seam_down)(down_step)

    def off_seam(up_step, down_step):
        pl.when(jnp.logical_and(has_up, jnp.logical_not(seam_up)))(up_step)
        pl.when(jnp.logical_and(has_down, jnp.logical_not(seam_down)))(down_step)

    def arrive(copies):
        return copies[1].wait_recv, copies[0].wait_recv

    def leave(copies):
        return copies[0].start, copies[1].start

    on_seam(*leave(gas_copies(whole + 1)))
    for n in range(whole + 1):
        start_both(gas_copies(n))
    off_seam(*leave(gas_copies(whole + 1)))

    top = pl.ds(rows, 8)
    bottom = pl.ds(8, 8)
    halo_low = pl.ds(0, 8)
    halo_high = pl.ds(rows + 8, 8)
    drow = (
        remote(fld.at[:, top, :], fld.at[:, halo_low, :], row_send.at[0], row_recv.at[0], up),
        remote(fld.at[:, bottom, :], fld.at[:, halo_high, :], row_send.at[1], row_recv.at[1], down),
    )
    prow = (
        remote(potp.at[top, :], prow_in.at[0], row_send.at[2], row_recv.at[2], up),
        remote(potp.at[bottom, :], prow_in.at[1], row_send.at[3], row_recv.at[3], down),
    )

    @pl.when(jnp.logical_not(has_down))
    def _():
        ext[0:rows, :] = jnp.zeros((rows, arc), BF16)
        gz[:, 0:rows, :] = jnp.zeros((2, rows, lead), BF16)
        fld[:, 0:8, :] = jnp.zeros((3, 8, arc), F32)
        prow_in[0] = jnp.zeros((8, arc), F32)

    @pl.when(jnp.logical_not(has_up))
    def _():
        ext[2 * rows : 3 * rows, :] = jnp.zeros((rows, arc), BF16)
        gz[:, 2 * rows : 3 * rows, :] = jnp.zeros((2, rows, lead), BF16)
        fld[:, rows + 8 : rows + 16, :] = jnp.zeros((3, 8, arc), F32)
        prow_in[1] = jnp.zeros((8, arc), F32)

    def col_copy(kind, d):
        where = side_two[d] if kind == 2 else side[d]
        return remote(
            col_out.at[kind, d],
            col_in.at[kind, d],
            col_send.at[d],
            col_recv.at[kind, d],
            {"sector": where},
        )

    def edge(tile, d):
        lane = 127 if d == 0 else 0
        return jnp.transpose(tile)[lane : lane + 1, :]

    def edge_tile(d):
        return slice(arc - 128, arc) if d == 0 else slice(0, 128)

    for copy in load_fields:
        copy.wait()
    for d in range(2):
        for n in range(3):
            col_out[0, d, n : n + 1, :] = edge(fld[n, 8 : 8 + rows, edge_tile(d)], d)
        col_copy(0, d).start()

    def far_copy(d, n):
        if n < whole:
            part, cols = pl.ds(0, rows), pl.ds(*pieces[n])
        else:
            part, cols = pl.ds((n - whole) * chunk, chunk), pl.ds(*pieces[whole])
        return remote(
            far_out.at[d, part, cols],
            far_in.at[d, part, cols],
            far_send.at[d],
            far_recv.at[d, n],
            {"sector": side[d]},
        )

    rim = 16

    def span(c):
        if c >= chunks:
            return (0, rim) if c == chunks else (rows - rim, rim)
        low = c * chunk + (rim if c == 0 else 0)
        return low, (c + 1) * chunk - (rim if c == chunks - 1 else 0) - low

    def part_copy(d, c):
        part = pl.ds(*span(c))
        return remote(
            part_out.at[d, part, :],
            part_in.at[d, part, :],
            part_send.at[d],
            part_recv.at[d, min(c, chunks)],
            {"sector": side[d]},
        )

    order = [(chunks - n) % chunks for n in range(chunks)]
    load_gas.wait()
    load_gr[4].wait()
    load_gr[0].wait()
    def pass_on():
        for d in range(2):
            first_own(d).wait()
            off_seam(first_on(d, 0).start, first_on(d, 2).start)

    early = jnp.logical_or(lax.rem(band, 2) == 1, seam_down)
    pl.when(early)(pass_on)
    on_seam(*arrive(gas_copies(whole + 1)))
    for d in range(2):
        on_seam(first_seam(d, 2).start, first_seam(d, 0).start)

    for n in range(whole):
        both(*arrive(gas_copies(n)))
        cols = slice(pieces[n][0], pieces[n][0] + pieces[n][1])
        for d, j in ((0, 4), (1, 0)):
            far_out[d, :, cols] = jnp.dot(
                gr[j], ext[:, cols], preferred_element_type=F32
            ).astype(BF16)
            far_copy(d, n).start()
    pl.when(jnp.logical_not(early))(pass_on)
    both(*arrive(gas_copies(whole)))
    last = slice(pieces[whole][0], pieces[whole][0] + pieces[whole][1])
    for c in order:
        part = slice(c * chunk, (c + 1) * chunk)
        for d, j in ((0, 4), (1, 0)):
            far_out[d, part, last] = jnp.dot(
                gr[j, part, :], ext[:, last], preferred_element_type=F32
            ).astype(BF16)
            far_copy(d, whole + c).start()

    start_both(drow)
    off_seam(*arrive(gas_copies(whole + 1)))
    load_inner.wait()
    load_ga.wait()
    for d, j in ((0, 3), (1, 1)):
        near[d] = jnp.dot(gr[j], ext[...], preferred_element_type=F32).astype(BF16)

    for d, j in ((0, 4), (1, 0)):

        @pl.when(has_up)
        def _():
            first_on(d, 0).wait_send()
            first_on(d, 2).wait_recv()

        @pl.when(has_down)
        def _():
            first_on(d, 2).wait_send()
            first_on(d, 0).wait_recv()

        far_in[d, :, 0:lead] = jnp.dot(gr[j], gz[d], preferred_element_type=F32).astype(BF16)
    for d in range(2):
        for n in range(whole):
            far_copy(d, n).wait_recv()
    for c in order:
        part = slice(c * chunk, (c + 1) * chunk)
        for d, j in ((0, 3), (1, 1)):
            far_copy(d, whole + c).wait_recv()
            total = jnp.dot(near[d, part, :], ga[j], preferred_element_type=F32) + jnp.dot(
                far_in[d, part, :], ga[4 - 4 * d], preferred_element_type=F32
            )
            part_out[d, part, :] = total.astype(BF16)
            if c == 0:
                part_copy(d, chunks).start()
            if c == chunks - 1:
                part_copy(d, chunks + 1).start()
            part_copy(d, c).start()

    for d in range(2):
        col_out[2, d, 0:1, :] = edge(part_out[d, :, edge_tile(d)].astype(F32), d)
        col_copy(2, d).start()
        col_own[1 - d, 0:1, :] = edge(part_out[d, :, edge_tile(1 - d)].astype(F32), 1 - d)

    middle = jnp.dot(gr[2], ext[...], preferred_element_type=F32).astype(BF16)
    potp[body_rows, :] = jnp.dot(middle, ga[2], preferred_element_type=F32)
    for d in range(2):
        col_out[1, d, 0:1, :] = edge(potp[8 : 8 + rows, edge_tile(d)], d)
        col_copy(1, d).start()

    load_k.wait()
    for d in range(2):
        col_copy(0, d).wait_recv()
    wait_both(drow)

    def columns(block):
        return jnp.transpose(jnp.concatenate([block, jnp.zeros((120, rows), F32)], axis=0))

    for d in range(2):
        dcol[d] = columns(col_in[0, d])

    def dust(start, stop):
        lanes = lax.broadcasted_iota(jnp.int32, (strip, arc), 1)
        is_first = lanes == 0
        is_last = lanes == arc - 1

        @pl.loop(start // strip, stop // strip)
        def _(step):
            first = pl.multiple_of(step * strip, strip)
            part = pl.ds(first, strip)
            window = pl.ds(first, strip + 16)
            inv = inverse_radius(band * rows + first, strip, rows * bands)
            west_edge = dcol[0, part, :]
            east_edge = dcol[1, part, :]
            centre, above, below, east, west = [], [], [], [], []
            for n in range(3):
                q = fld[n, window, :]
                mid = q[8 : 8 + strip]
                centre.append(mid)
                above.append(q[9 : 9 + strip])
                below.append(q[7 : 7 + strip])
                east.append(
                    jnp.where(is_last, east_edge[:, n : n + 1], pltpu.roll(mid, arc - 1, 1))
                )
                west.append(jnp.where(is_first, west_edge[:, n : n + 1], pltpu.roll(mid, 1, 1)))
            rho, u, w = centre
            k = kv[part, :].astype(F32)
            lap = [above[n] + below[n] + east[n] + west[n] - 4.0 * centre[n] for n in range(3)]
            density_next[part, :] = (
                rho
                - 0.5 * (above[0] * above[1] - below[0] * below[1])
                - 0.5 * inv * (east[0] * east[2] - west[0] * west[2])
                + diffusion * lap[0]
            )
            radial_next[part, :] = (
                u
                - 0.5 * u * (above[1] - below[1])
                - 0.5 * inv * w * (east[1] - west[1])
                - k * u
                + diffusion * lap[1]
            )
            azimuth_next[part, :] = (
                w
                - 0.5 * u * (above[2] - below[2])
                - 0.5 * inv * w * (east[2] - west[2])
                - k * (w - kepler * jnp.sqrt(inv))
                + diffusion * lap[2]
            )

    def settle(low, count):
        part = slice(low, low + count)
        here = slice(8 + low, 8 + low + count)
        potp[here, :] = potp[here, :] + (
            part_in[0, part, :].astype(F32) + part_in[1, part, :].astype(F32)
        )

    for d in range(2):
        both_rims = pl.ds(0, 2 * rim)
        remote(
            part_out.at[d, both_rims, :],
            part_in.at[d, both_rims, :],
            part_send.at[d],
            part_recv.at[d, chunks],
            {"sector": side[d]},
        ).wait_recv()
    settle(0, rim)
    settle(rows - rim, rim)
    start_both(prow)

    dust(0, rows)

    for d in range(2):
        col_copy(1, d).wait_recv()
        col_copy(2, d).wait_recv()
        row = col_in[1, d, 0:1, :] + (col_in[2, d, 0:1, :] + col_own[d, 0:1, :])
        edges[d] = jnp.transpose(jnp.concatenate([row, jnp.zeros((127, rows), F32)], axis=0))

    for c in order:
        for d in range(2):
            part_copy(d, c).wait_recv()
        settle(*span(c))
    wait_both(prow)
    potp[0:8, :] = prow_in[0]
    potp[rows + 8 : rows + 16, :] = prow_in[1]

    sent_cols = pl.ds(lead, arc - lead)
    for d in range(2):
        where = {"sector": side[d]}
        remote(
            far_out.at[d, :, sent_cols],
            far_in.at[d, :, sent_cols],
            far_send.at[d],
            far_recv.at[d, 0],
            where,
        ).wait_send()
        remote(
            part_out.at[d], part_in.at[d], part_send.at[d], part_recv.at[d, 0], where
        ).wait_send()
        remote(
            col_out.at[:, d], col_in.at[:, d], col_send.at[d], col_recv.at[0, d], where
        ).wait_send()
    both(
        remote(gas, ext.at[thirds[0], :], gas_send.at[0], gas_recv.at[0, 0], up).wait_send,
        remote(gas, ext.at[thirds[2], :], gas_send.at[1], gas_recv.at[1, 0], down).wait_send,
    )


def finish(
    chunk,
    potp,
    edges,
    density_part,
    radial_part,
    azimuth_part,
    potential,
    density_next,
    radial_next,
    azimuth_next,
    radial,
    azimuth,
    sem,
):
    rows, arc = density_part.shape
    band = lax.axis_index("band")
    total_rows = rows * lax.axis_size("band")
    copies = [
        pltpu.make_async_copy(density_part, density_next, sem.at[0]),
        pltpu.make_async_copy(potp.at[pl.ds(8, rows), :], potential, sem.at[1]),
    ]
    for copy in copies:
        copy.start()
    lanes = lax.broadcasted_iota(jnp.int32, (chunk, arc), 1)
    is_first = lanes == 0
    is_last = lanes == arc - 1
    for c in range(rows // chunk):
        part = slice(c * chunk, (c + 1) * chunk)
        cut = pl.ds(c * chunk, chunk)
        q = potp[c * chunk : (c + 1) * chunk + 16, :]
        radial[part, :] = radial_part[part, :] - 0.5 * gravity * (
            q[9 : 9 + chunk] - q[7 : 7 + chunk]
        )
        copies.append(
            pltpu.make_async_copy(radial.at[cut, :], radial_next.at[cut, :], sem.at[2 + 2 * c])
        )
        copies[-1].start()
        mid = q[8 : 8 + chunk]
        inv = inverse_radius(band * rows + c * chunk, chunk, total_rows)
        east = jnp.where(is_last, edges[1, part, 0:1], pltpu.roll(mid, arc - 1, 1))
        west = jnp.where(is_first, edges[0, part, 0:1], pltpu.roll(mid, 1, 1))
        azimuth[part, :] = azimuth_part[part, :] - 0.5 * gravity * inv * (east - west)
        copies.append(
            pltpu.make_async_copy(azimuth.at[cut, :], azimuth_next.at[cut, :], sem.at[3 + 2 * c])
        )
        copies[-1].start()
    for copy in copies:
        copy.wait()


def body(gas, green_radial, green_azimuth, rho, u, w, coupling, chunk, strip, pieces):
    lead = pieces[-1][1]
    rows, arc = rho.shape
    chunks = rows // chunk
    steps = len(pieces)
    dma = pltpu.SemaphoreType.DMA
    operands = (gas, green_radial, green_azimuth, rho, u, w, coupling)
    results = pl.pallas_call(
        functools.partial(kernel, chunk, strip, pieces),
        out_shape=[
            pltpu.VMEM((rows + 16, arc), F32),
            pltpu.VMEM((2, rows, 128), F32),
        ]
        + [pltpu.VMEM((rows, arc), F32)] * 3,
        in_specs=[pl.BlockSpec(memory_space=pltpu.HBM)] * 7,
        out_specs=[pl.BlockSpec(memory_space=pltpu.VMEM)] * 5,
        scratch_shapes=[
            pltpu.VMEM((3 * rows, arc), BF16),
            pltpu.VMEM((2, 3 * rows, lead), BF16),
            pltpu.VMEM((5, rows, 3 * rows), BF16),
            pltpu.VMEM((5, arc, arc), BF16),
            pltpu.VMEM((3, rows + 16, arc), F32),
            pltpu.VMEM((rows, arc), BF16),
            pltpu.VMEM((2, 8, arc), F32),
            pltpu.VMEM((2, rows, arc), BF16),
            pltpu.VMEM((2, rows, arc), BF16),
            pltpu.VMEM((2, rows, arc), BF16),
            pltpu.VMEM((2, rows, arc), BF16),
            pltpu.VMEM((2, rows, arc), BF16),
            pltpu.VMEM((3, 2, 8, rows), F32),
            pltpu.VMEM((3, 2, 8, rows), F32),
            pltpu.VMEM((2, 8, rows), F32),
            pltpu.VMEM((2, rows, 128), F32),
            dma((9,)),
            dma((2,)),
            dma((2, steps)),
            dma((2, 3)),
            dma((2, 3)),
            dma((4,)),
            dma((4,)),
            dma((2,)),
            dma((3, 2)),
            dma((2,)),
            dma((2, steps - 2 + chunks)),
            dma((2,)),
            dma((2, chunks + 1)),
        ],
        compiler_params=pltpu.CompilerParams(
            collective_id=0, has_side_effects=True, vmem_limit_bytes=50 * 2**20
        ),
        name="disc",
    )(*[pltpu.with_memory_space_constraint(x, pltpu.HBM) for x in operands])
    return pl.pallas_call(
        functools.partial(finish, chunk),
        out_shape=[jax.ShapeDtypeStruct((rows, arc), F32)] * 4,
        in_specs=[pl.BlockSpec(memory_space=pltpu.VMEM)] * 5,
        out_specs=[pl.BlockSpec(memory_space=pl.ANY)] * 4,
        scratch_shapes=[
            pltpu.VMEM((rows, arc), F32),
            pltpu.VMEM((rows, arc), F32),
            dma((2 + 2 * chunks,)),
        ],
        compiler_params=pltpu.CompilerParams(vmem_limit_bytes=4 * 2**20),
        name="finish",
    )(*[pltpu.with_memory_space_constraint(r, pltpu.VMEM) for r in results])


def solution(mesh, chunk=96, strip=32, pieces=((128, 128), (256, 256), (0, 128))):
    return jax.shard_map(
        functools.partial(body, chunk=chunk, strip=strip, pieces=pieces),
        mesh=mesh,
        in_specs=(
            P("band", "sector"),
            P(None, "band", None),
            P(),
            P("band", "sector"),
            P("band", "sector"),
            P("band", "sector"),
            P("band", "sector"),
        ),
        out_specs=(P("band", "sector"),) * 4,
        check_vma=False,
    )
```

```python
import functools

import jax
import jax.numpy as jnp
from jax import lax
from jax.experimental import pallas as pl
from jax.experimental.pallas import tpu as pltpu
from jax.sharding import PartitionSpec as P

diffusion = 0.1
gravity = 0.1
kepler = 0.6

MESH = pl.DeviceIdType.MESH
F32 = jnp.float32
BF16 = jnp.bfloat16


def inverse_radius(first, count, total_rows):
    index = first + lax.broadcasted_iota(jnp.int32, (count, 1), 0)
    return 1.0 / (1.0 + 3.0 * (index.astype(F32) + 0.5) / total_rows)


def kernel(
    chunk,
    strip,
    pieces,
    gas,
    green_radial,
    green_azimuth,
    dust_density,
    dust_radial,
    dust_azimuth,
    coupling,
    potp,
    edges,
    density_next,
    radial_next,
    azimuth_next,
    ext,
    gz,
    hop,
    gr,
    ga,
    fld,
    kv,
    prow_in,
    near,
    far_out,
    far_in,
    part_out,
    part_in,
    col_out,
    col_in,
    col_own,
    dcol,
    load_sem,
    gas_send,
    gas_recv,
    first_send,
    first_recv,
    hop_sem,
    row_send,
    row_recv,
    col_send,
    col_recv,
    far_send,
    far_recv,
    part_send,
    part_recv,
):
    rows, arc = dust_density.shape
    chunks = rows // chunk
    band = lax.axis_index("band")
    sector = lax.axis_index("sector")
    bands = lax.axis_size("band")
    sectors = lax.axis_size("sector")
    side = (lax.rem(sector + 1, sectors), lax.rem(sector + sectors - 1, sectors))
    side_two = (lax.rem(sector + 2, sectors), lax.rem(sector + sectors - 2, sectors))
    has_up = band < bands - 1
    has_down = band > 0
    seam_up = band == bands // 2 - 1
    seam_down = band == bands // 2
    seam = jnp.logical_or(seam_up, seam_down)
    end = jnp.logical_or(band == 0, band == bands - 1)

    lead = gz.shape[2]
    whole = len(pieces) - 2

    def load(src, dst, n):
        copy = pltpu.make_async_copy(src, dst, load_sem.at[n])
        copy.start()
        return copy

    own = pl.ds(rows, rows)
    body_rows = pl.ds(8, rows)
    load_gas = load(gas, ext.at[own, :], 3)
    load_gr = {}
    for n, j in enumerate((4, 0)):
        load_gr[j] = load(green_radial.at[j], gr.at[j], 4 + n)
    load_fields = [
        load(field, fld.at[n, body_rows, :], n)
        for n, field in enumerate((dust_density, dust_radial, dust_azimuth))
    ]
    load_inner = load(green_radial.at[pl.ds(1, 3)], gr.at[pl.ds(1, 3)], 6)
    load_ga = load(green_azimuth, ga, 7)
    load_k = load(coupling, kv, 8)

    barrier = pltpu.get_barrier_semaphore()
    for s in side + side_two:
        pl.semaphore_signal(barrier, inc=1, device_id={"sector": s}, device_id_type=MESH)

    @pl.when(has_up)
    def _():
        pl.semaphore_signal(barrier, inc=1, device_id={"band": band + 1}, device_id_type=MESH)

    @pl.when(has_down)
    def _():
        pl.semaphore_signal(barrier, inc=1, device_id={"band": band - 1}, device_id_type=MESH)

    @pl.when(seam)
    def _():
        for b in (0, bands - 1):
            pl.semaphore_signal(barrier, inc=1, device_id={"band": b}, device_id_type=MESH)

    @pl.when(end)
    def _():
        for b in (bands // 2 - 1, bands // 2):
            pl.semaphore_signal(barrier, inc=1, device_id={"band": b}, device_id_type=MESH)

    pl.semaphore_wait(
        barrier,
        4
        + has_up.astype(jnp.int32)
        + has_down.astype(jnp.int32)
        + 2 * seam.astype(jnp.int32)
        + 2 * end.astype(jnp.int32),
    )

    def remote(src, dst, send, recv, where):
        return pltpu.make_async_remote_copy(
            src_ref=src,
            dst_ref=dst,
            send_sem=send,
            recv_sem=recv,
            device_id=where,
            device_id_type=MESH,
        )

    up = {"band": band + 1}
    down = {"band": band - 1}

    def gas_copies(n, part=None):
        cols = pl.ds(*(part or pieces[n]))
        return (
            remote(
                gas.at[:, cols],
                ext.at[pl.ds(0, rows), cols],
                gas_send.at[0],
                gas_recv.at[0, n],
                up,
            ),
            remote(
                gas.at[:, cols],
                ext.at[pl.ds(2 * rows, rows), cols],
                gas_send.at[1],
                gas_recv.at[1, n],
                down,
            ),
        )

    def both(up_step, down_step):
        pl.when(has_up)(up_step)
        pl.when(has_down)(down_step)

    def start_both(copies):
        both(copies[0].start, copies[1].start)

    def wait_both(copies):
        @pl.when(has_up)
        def _():
            copies[0].wait_send()
            copies[1].wait_recv()

        @pl.when(has_down)
        def _():
            copies[1].wait_send()
            copies[0].wait_recv()

    thirds = [pl.ds(n * rows, rows) for n in range(3)]

    def first_copy(d, third, src, where, sent):
        return remote(
            src, gz.at[d, thirds[third], :], first_send.at[d, sent], first_recv.at[d, third], where
        )

    head = pl.ds(0, lead)

    def first_own(d):
        return first_copy(d, 1, gas.at[:, head], {"sector": side[d]}, 1)

    def first_on(d, third):
        where = up if third == 0 else down
        return first_copy(d, third, gz.at[d, thirds[1], :], where, third)

    def first_seam(d, third):
        return first_copy(d, third, ext.at[thirds[third], head], {"sector": side[d]}, 2 - third)

    for d in range(2):
        first_own(d).start()
    def on_seam(up_step, down_step):
        pl.when(seam_up)(up_step)
        pl.when(seam_down)(down_step)

    def off_seam(up_step, down_step):
        pl.when(jnp.logical_and(has_up, jnp.logical_not(seam_up)))(up_step)
        pl.when(jnp.logical_and(has_down, jnp.logical_not(seam_down)))(down_step)

    def arrive(copies):
        return copies[1].wait_recv, copies[0].wait_recv

    def leave(copies):
        return copies[0].start, copies[1].start

    first_col, count = pieces[whole]
    straight = (first_col, count // 2)
    around = pl.ds(first_col + count // 2, count // 2)
    out_up = remote(
        gas.at[:, around], hop, gas_send.at[0], hop_sem.at[0], {"band": bands - 1}
    )
    out_down = remote(gas.at[:, around], hop, gas_send.at[1], hop_sem.at[0], {"band": 0})
    on_up = remote(
        hop, ext.at[pl.ds(0, rows), around], hop_sem.at[1], hop_sem.at[2], {"band": bands // 2}
    )
    on_down = remote(
        hop,
        ext.at[pl.ds(2 * rows, rows), around],
        hop_sem.at[1],
        hop_sem.at[2],
        {"band": bands // 2 - 1},
    )

    on_seam(*leave(gas_copies(whole + 1)))
    on_seam(out_up.start, out_down.start)
    for n in range(whole):
        start_both(gas_copies(n))
    on_seam(*leave(gas_copies(whole, straight)))
    off_seam(*leave(gas_copies(whole)))
    off_seam(*leave(gas_copies(whole + 1)))

    top = pl.ds(rows, 8)
    bottom = pl.ds(8, 8)
    halo_low = pl.ds(0, 8)
    halo_high = pl.ds(rows + 8, 8)
    drow = (
        remote(fld.at[:, top, :], fld.at[:, halo_low, :], row_send.at[0], row_recv.at[0], up),
        remote(fld.at[:, bottom, :], fld.at[:, halo_high, :], row_send.at[1], row_recv.at[1], down),
    )
    prow = (
        remote(potp.at[top, :], prow_in.at[0], row_send.at[2], row_recv.at[2], up),
        remote(potp.at[bottom, :], prow_in.at[1], row_send.at[3], row_recv.at[3], down),
    )

    @pl.when(jnp.logical_not(has_down))
    def _():
        ext[0:rows, :] = jnp.zeros((rows, arc), BF16)
        gz[:, 0:rows, :] = jnp.zeros((2, rows, lead), BF16)
        fld[:, 0:8, :] = jnp.zeros((3, 8, arc), F32)
        prow_in[0] = jnp.zeros((8, arc), F32)

    @pl.when(jnp.logical_not(has_up))
    def _():
        ext[2 * rows : 3 * rows, :] = jnp.zeros((rows, arc), BF16)
        gz[:, 2 * rows : 3 * rows, :] = jnp.zeros((2, rows, lead), BF16)
        fld[:, rows + 8 : rows + 16, :] = jnp.zeros((3, 8, arc), F32)
        prow_in[1] = jnp.zeros((8, arc), F32)

    def col_copy(kind, d):
        where = side_two[d] if kind == 2 else side[d]
        return remote(
            col_out.at[kind, d],
            col_in.at[kind, d],
            col_send.at[d],
            col_recv.at[kind, d],
            {"sector": where},
        )

    def edge(tile, d):
        lane = 127 if d == 0 else 0
        return jnp.transpose(tile)[lane : lane + 1, :]

    def edge_tile(d):
        return slice(arc - 128, arc) if d == 0 else slice(0, 128)

    for copy in load_fields:
        copy.wait()
    for d in range(2):
        for n in range(3):
            col_out[0, d, n : n + 1, :] = edge(fld[n, 8 : 8 + rows, edge_tile(d)], d)
        col_copy(0, d).start()

    def far_copy(d, n):
        if n < whole:
            part, cols = pl.ds(0, rows), pl.ds(*pieces[n])
        else:
            part, cols = pl.ds((n - whole) * chunk, chunk), pl.ds(*pieces[whole])
        return remote(
            far_out.at[d, part, cols],
            far_in.at[d, part, cols],
            far_send.at[d],
            far_recv.at[d, n],
            {"sector": side[d]},
        )

    rim = 16

    def span(c):
        if c >= chunks:
            return (0, rim) if c == chunks else (rows - rim, rim)
        low = c * chunk + (rim if c == 0 else 0)
        return low, (c + 1) * chunk - (rim if c == chunks - 1 else 0) - low

    def part_copy(d, c):
        part = pl.ds(*span(c))
        return remote(
            part_out.at[d, part, :],
            part_in.at[d, part, :],
            part_send.at[d],
            part_recv.at[d, min(c, chunks)],
            {"sector": side[d]},
        )

    order = [(chunks - n) % chunks for n in range(chunks)]
    load_gas.wait()
    load_gr[4].wait()
    load_gr[0].wait()
    def pass_on():
        for d in range(2):
            first_own(d).wait()
            off_seam(first_on(d, 0).start, first_on(d, 2).start)

    early = jnp.logical_or(lax.rem(band, 2) == 1, seam_down)
    pl.when(early)(pass_on)
    on_seam(*arrive(gas_copies(whole + 1)))
    for d in range(2):
        on_seam(first_seam(d, 2).start, first_seam(d, 0).start)

    for n in range(whole):
        both(*arrive(gas_copies(n)))
        cols = slice(pieces[n][0], pieces[n][0] + pieces[n][1])
        for d, j in ((0, 4), (1, 0)):
            far_out[d, :, cols] = jnp.dot(
                gr[j], ext[:, cols], preferred_element_type=F32
            ).astype(BF16)
            far_copy(d, n).start()
    pl.when(jnp.logical_not(early))(pass_on)
    @pl.when(band == bands - 1)
    def _():
        out_up.wait_recv()
        on_up.start()

    @pl.when(band == 0)
    def _():
        out_down.wait_recv()
        on_down.start()

    off_seam(*arrive(gas_copies(whole)))
    on_seam(*arrive(gas_copies(whole, straight)))
    on_seam(on_down.wait_recv, on_up.wait_recv)
    last = slice(pieces[whole][0], pieces[whole][0] + pieces[whole][1])
    for c in order:
        part = slice(c * chunk, (c + 1) * chunk)
        for d, j in ((0, 4), (1, 0)):
            far_out[d, part, last] = jnp.dot(
                gr[j, part, :], ext[:, last], preferred_element_type=F32
            ).astype(BF16)
            far_copy(d, whole + c).start()

    start_both(drow)
    off_seam(*arrive(gas_copies(whole + 1)))
    load_inner.wait()
    load_ga.wait()
    for d, j in ((0, 3), (1, 1)):
        near[d] = jnp.dot(gr[j], ext[...], preferred_element_type=F32).astype(BF16)

    for d, j in ((0, 4), (1, 0)):

        @pl.when(has_up)
        def _():
            first_on(d, 0).wait_send()
            first_on(d, 2).wait_recv()

        @pl.when(has_down)
        def _():
            first_on(d, 2).wait_send()
            first_on(d, 0).wait_recv()

        far_in[d, :, 0:lead] = jnp.dot(gr[j], gz[d], preferred_element_type=F32).astype(BF16)
    for d in range(2):
        for n in range(whole):
            far_copy(d, n).wait_recv()
    for c in order:
        part = slice(c * chunk, (c + 1) * chunk)
        for d, j in ((0, 3), (1, 1)):
            far_copy(d, whole + c).wait_recv()
            total = jnp.dot(near[d, part, :], ga[j], preferred_element_type=F32) + jnp.dot(
                far_in[d, part, :], ga[4 - 4 * d], preferred_element_type=F32
            )
            part_out[d, part, :] = total.astype(BF16)
            if c == 0:
                part_copy(d, chunks).start()
            if c == chunks - 1:
                part_copy(d, chunks + 1).start()
            part_copy(d, c).start()

    for d in range(2):
        col_out[2, d, 0:1, :] = edge(part_out[d, :, edge_tile(d)].astype(F32), d)
        col_copy(2, d).start()
        col_own[1 - d, 0:1, :] = edge(part_out[d, :, edge_tile(1 - d)].astype(F32), 1 - d)

    middle = jnp.dot(gr[2], ext[...], preferred_element_type=F32).astype(BF16)
    potp[body_rows, :] = jnp.dot(middle, ga[2], preferred_element_type=F32)
    for d in range(2):
        col_out[1, d, 0:1, :] = edge(potp[8 : 8 + rows, edge_tile(d)], d)
        col_copy(1, d).start()

    load_k.wait()
    for d in range(2):
        col_copy(0, d).wait_recv()
    wait_both(drow)

    def columns(block):
        return jnp.transpose(jnp.concatenate([block, jnp.zeros((120, rows), F32)], axis=0))

    for d in range(2):
        dcol[d] = columns(col_in[0, d])

    def dust(start, stop):
        lanes = lax.broadcasted_iota(jnp.int32, (strip, arc), 1)
        is_first = lanes == 0
        is_last = lanes == arc - 1

        @pl.loop(start // strip, stop // strip)
        def _(step):
            first = pl.multiple_of(step * strip, strip)
            part = pl.ds(first, strip)
            window = pl.ds(first, strip + 16)
            inv = inverse_radius(band * rows + first, strip, rows * bands)
            west_edge = dcol[0, part, :]
            east_edge = dcol[1, part, :]
            centre, above, below, east, west = [], [], [], [], []
            for n in range(3):
                q = fld[n, window, :]
                mid = q[8 : 8 + strip]
                centre.append(mid)
                above.append(q[9 : 9 + strip])
                below.append(q[7 : 7 + strip])
                east.append(
                    jnp.where(is_last, east_edge[:, n : n + 1], pltpu.roll(mid, arc - 1, 1))
                )
                west.append(jnp.where(is_first, west_edge[:, n : n + 1], pltpu.roll(mid, 1, 1)))
            rho, u, w = centre
            k = kv[part, :].astype(F32)
            lap = [above[n] + below[n] + east[n] + west[n] - 4.0 * centre[n] for n in range(3)]
            density_next[part, :] = (
                rho
                - 0.5 * (above[0] * above[1] - below[0] * below[1])
                - 0.5 * inv * (east[0] * east[2] - west[0] * west[2])
                + diffusion * lap[0]
            )
            radial_next[part, :] = (
                u
                - 0.5 * u * (above[1] - below[1])
                - 0.5 * inv * w * (east[1] - west[1])
                - k * u
                + diffusion * lap[1]
            )
            azimuth_next[part, :] = (
                w
                - 0.5 * u * (above[2] - below[2])
                - 0.5 * inv * w * (east[2] - west[2])
                - k * (w - kepler * jnp.sqrt(inv))
                + diffusion * lap[2]
            )

    def settle(low, count):
        part = slice(low, low + count)
        here = slice(8 + low, 8 + low + count)
        potp[here, :] = potp[here, :] + (
            part_in[0, part, :].astype(F32) + part_in[1, part, :].astype(F32)
        )

    for d in range(2):
        both_rims = pl.ds(0, 2 * rim)
        remote(
            part_out.at[d, both_rims, :],
            part_in.at[d, both_rims, :],
            part_send.at[d],
            part_recv.at[d, chunks],
            {"sector": side[d]},
        ).wait_recv()
    settle(0, rim)
    settle(rows - rim, rim)
    start_both(prow)

    dust(0, rows)

    for d in range(2):
        col_copy(1, d).wait_recv()
        col_copy(2, d).wait_recv()
        row = col_in[1, d, 0:1, :] + (col_in[2, d, 0:1, :] + col_own[d, 0:1, :])
        edges[d] = jnp.transpose(jnp.concatenate([row, jnp.zeros((127, rows), F32)], axis=0))

    for c in order:
        for d in range(2):
            part_copy(d, c).wait_recv()
        settle(*span(c))
    wait_both(prow)
    potp[0:8, :] = prow_in[0]
    potp[rows + 8 : rows + 16, :] = prow_in[1]

    pl.when(band == bands - 1)(on_up.wait_send)
    pl.when(band == 0)(on_down.wait_send)
    sent_cols = pl.ds(lead, arc - lead)
    for d in range(2):
        where = {"sector": side[d]}
        remote(
            far_out.at[d, :, sent_cols],
            far_in.at[d, :, sent_cols],
            far_send.at[d],
            far_recv.at[d, 0],
            where,
        ).wait_send()
        remote(
            part_out.at[d], part_in.at[d], part_send.at[d], part_recv.at[d, 0], where
        ).wait_send()
        remote(
            col_out.at[:, d], col_in.at[:, d], col_send.at[d], col_recv.at[0, d], where
        ).wait_send()
    both(
        remote(gas, ext.at[thirds[0], :], gas_send.at[0], gas_recv.at[0, 0], up).wait_send,
        remote(gas, ext.at[thirds[2], :], gas_send.at[1], gas_recv.at[1, 0], down).wait_send,
    )


def finish(
    chunk,
    potp,
    edges,
    density_part,
    radial_part,
    azimuth_part,
    potential,
    density_next,
    radial_next,
    azimuth_next,
    radial,
    azimuth,
    sem,
):
    rows, arc = density_part.shape
    band = lax.axis_index("band")
    total_rows = rows * lax.axis_size("band")
    copies = [
        pltpu.make_async_copy(density_part, density_next, sem.at[0]),
        pltpu.make_async_copy(potp.at[pl.ds(8, rows), :], potential, sem.at[1]),
    ]
    for copy in copies:
        copy.start()
    lanes = lax.broadcasted_iota(jnp.int32, (chunk, arc), 1)
    is_first = lanes == 0
    is_last = lanes == arc - 1
    for c in range(rows // chunk):
        part = slice(c * chunk, (c + 1) * chunk)
        cut = pl.ds(c * chunk, chunk)
        q = potp[c * chunk : (c + 1) * chunk + 16, :]
        radial[part, :] = radial_part[part, :] - 0.5 * gravity * (
            q[9 : 9 + chunk] - q[7 : 7 + chunk]
        )
        copies.append(
            pltpu.make_async_copy(radial.at[cut, :], radial_next.at[cut, :], sem.at[2 + 2 * c])
        )
        copies[-1].start()
        mid = q[8 : 8 + chunk]
        inv = inverse_radius(band * rows + c * chunk, chunk, total_rows)
        east = jnp.where(is_last, edges[1, part, 0:1], pltpu.roll(mid, arc - 1, 1))
        west = jnp.where(is_first, edges[0, part, 0:1], pltpu.roll(mid, 1, 1))
        azimuth[part, :] = azimuth_part[part, :] - 0.5 * gravity * inv * (east - west)
        copies.append(
            pltpu.make_async_copy(azimuth.at[cut, :], azimuth_next.at[cut, :], sem.at[3 + 2 * c])
        )
        copies[-1].start()
    for copy in copies:
        copy.wait()


def body(gas, green_radial, green_azimuth, rho, u, w, coupling, chunk, strip, pieces):
    lead = pieces[-1][1]
    rows, arc = rho.shape
    chunks = rows // chunk
    steps = len(pieces)
    dma = pltpu.SemaphoreType.DMA
    operands = (gas, green_radial, green_azimuth, rho, u, w, coupling)
    results = pl.pallas_call(
        functools.partial(kernel, chunk, strip, pieces),
        out_shape=[
            pltpu.VMEM((rows + 16, arc), F32),
            pltpu.VMEM((2, rows, 128), F32),
        ]
        + [pltpu.VMEM((rows, arc), F32)] * 3,
        in_specs=[pl.BlockSpec(memory_space=pltpu.HBM)] * 7,
        out_specs=[pl.BlockSpec(memory_space=pltpu.VMEM)] * 5,
        scratch_shapes=[
            pltpu.VMEM((3 * rows, arc), BF16),
            pltpu.VMEM((2, 3 * rows, lead), BF16),
            pltpu.VMEM((rows, pieces[-2][1] // 2), BF16),
            pltpu.VMEM((5, rows, 3 * rows), BF16),
            pltpu.VMEM((5, arc, arc), BF16),
            pltpu.VMEM((3, rows + 16, arc), F32),
            pltpu.VMEM((rows, arc), BF16),
            pltpu.VMEM((2, 8, arc), F32),
            pltpu.VMEM((2, rows, arc), BF16),
            pltpu.VMEM((2, rows, arc), BF16),
            pltpu.VMEM((2, rows, arc), BF16),
            pltpu.VMEM((2, rows, arc), BF16),
            pltpu.VMEM((2, rows, arc), BF16),
            pltpu.VMEM((3, 2, 8, rows), F32),
            pltpu.VMEM((3, 2, 8, rows), F32),
            pltpu.VMEM((2, 8, rows), F32),
            pltpu.VMEM((2, rows, 128), F32),
            dma((9,)),
            dma((2,)),
            dma((2, steps)),
            dma((2, 3)),
            dma((2, 3)),
            dma((3,)),
            dma((4,)),
            dma((4,)),
            dma((2,)),
            dma((3, 2)),
            dma((2,)),
            dma((2, steps - 2 + chunks)),
            dma((2,)),
            dma((2, chunks + 1)),
        ],
        compiler_params=pltpu.CompilerParams(
            collective_id=0, has_side_effects=True, vmem_limit_bytes=50 * 2**20
        ),
        name="disc",
    )(*[pltpu.with_memory_space_constraint(x, pltpu.HBM) for x in operands])
    return pl.pallas_call(
        functools.partial(finish, chunk),
        out_shape=[jax.ShapeDtypeStruct((rows, arc), F32)] * 4,
        in_specs=[pl.BlockSpec(memory_space=pltpu.VMEM)] * 5,
        out_specs=[pl.BlockSpec(memory_space=pl.ANY)] * 4,
        scratch_shapes=[
            pltpu.VMEM((rows, arc), F32),
            pltpu.VMEM((rows, arc), F32),
            dma((2 + 2 * chunks,)),
        ],
        compiler_params=pltpu.CompilerParams(vmem_limit_bytes=4 * 2**20),
        name="finish",
    )(*[pltpu.with_memory_space_constraint(r, pltpu.VMEM) for r in results])


def solution(mesh, chunk=96, strip=32, pieces=((128, 128), (256, 256), (0, 128))):
    return jax.shard_map(
        functools.partial(body, chunk=chunk, strip=strip, pieces=pieces),
        mesh=mesh,
        in_specs=(
            P("band", "sector"),
            P(None, "band", None),
            P(),
            P("band", "sector"),
            P("band", "sector"),
            P("band", "sector"),
            P("band", "sector"),
        ),
        out_specs=(P("band", "sector"),) * 4,
        check_vma=False,
    )
```

```python
import functools

import jax
import jax.numpy as jnp
from jax import lax
from jax.experimental import pallas as pl
from jax.experimental.pallas import tpu as pltpu
from jax.sharding import PartitionSpec as P

diffusion = 0.1
gravity = 0.1
kepler = 0.6

MESH = pl.DeviceIdType.MESH
F32 = jnp.float32
BF16 = jnp.bfloat16


def inverse_radius(first, count, total_rows):
    index = first + lax.broadcasted_iota(jnp.int32, (count, 1), 0)
    return 1.0 / (1.0 + 3.0 * (index.astype(F32) + 0.5) / total_rows)


def kernel(
    chunk,
    strip,
    pieces,
    gas,
    green_radial,
    green_azimuth,
    dust_density,
    dust_radial,
    dust_azimuth,
    coupling,
    mid_pot,
    part_in,
    rims,
    edges,
    density_next,
    radial_next,
    azimuth_next,
    ext,
    gz,
    hop,
    gr,
    ga,
    fld,
    kv,
    prow_out,
    prow_in,
    near,
    far_out,
    far_in,
    part_out,
    col_out,
    col_in,
    col_own,
    dcol,
    load_sem,
    gas_send,
    gas_recv,
    first_send,
    first_recv,
    hop_sem,
    row_send,
    row_recv,
    col_send,
    col_recv,
    far_send,
    far_recv,
    part_send,
    part_recv,
):
    rows, arc = dust_density.shape
    chunks = rows // chunk
    band = lax.axis_index("band")
    sector = lax.axis_index("sector")
    bands = lax.axis_size("band")
    sectors = lax.axis_size("sector")
    side = (lax.rem(sector + 1, sectors), lax.rem(sector + sectors - 1, sectors))
    side_two = (lax.rem(sector + 2, sectors), lax.rem(sector + sectors - 2, sectors))
    has_up = band < bands - 1
    has_down = band > 0
    seam_up = band == bands // 2 - 1
    seam_down = band == bands // 2
    seam = jnp.logical_or(seam_up, seam_down)
    end = jnp.logical_or(band == 0, band == bands - 1)

    lead = gz.shape[2]
    whole = len(pieces) - 2

    barrier = pltpu.get_barrier_semaphore()
    for s in side + side_two:
        pl.semaphore_signal(barrier, inc=1, device_id={"sector": s}, device_id_type=MESH)

    @pl.when(has_up)
    def _():
        pl.semaphore_signal(barrier, inc=1, device_id={"band": band + 1}, device_id_type=MESH)

    @pl.when(has_down)
    def _():
        pl.semaphore_signal(barrier, inc=1, device_id={"band": band - 1}, device_id_type=MESH)

    @pl.when(seam)
    def _():
        for b in (0, bands - 1):
            pl.semaphore_signal(barrier, inc=1, device_id={"band": b}, device_id_type=MESH)

    @pl.when(end)
    def _():
        for b in (bands // 2 - 1, bands // 2):
            pl.semaphore_signal(barrier, inc=1, device_id={"band": b}, device_id_type=MESH)

    def load(src, dst, n):
        copy = pltpu.make_async_copy(src, dst, load_sem.at[n])
        copy.start()
        return copy

    own = pl.ds(rows, rows)
    body_rows = pl.ds(8, rows)
    load_gas = load(gas, ext.at[own, :], 3)
    load_gr = {}
    for n, j in enumerate((4, 0)):
        load_gr[j] = load(green_radial.at[j], gr.at[j], 4 + n)
    load_fields = [
        load(field, fld.at[n, body_rows, :], n)
        for n, field in enumerate((dust_density, dust_radial, dust_azimuth))
    ]
    load_inner = load(green_radial.at[pl.ds(1, 3)], gr.at[pl.ds(1, 3)], 6)
    load_ga = load(green_azimuth, ga, 7)
    load_k = load(coupling, kv, 8)

    load_gas.wait()
    pl.semaphore_wait(
        barrier,
        4
        + has_up.astype(jnp.int32)
        + has_down.astype(jnp.int32)
        + 2 * seam.astype(jnp.int32)
        + 2 * end.astype(jnp.int32),
    )

    def remote(src, dst, send, recv, where):
        return pltpu.make_async_remote_copy(
            src_ref=src,
            dst_ref=dst,
            send_sem=send,
            recv_sem=recv,
            device_id=where,
            device_id_type=MESH,
        )

    up = {"band": band + 1}
    down = {"band": band - 1}

    def gas_copies(n, part=None):
        cols = pl.ds(*(part or pieces[n]))
        return (
            remote(
                ext.at[own, cols],
                ext.at[pl.ds(0, rows), cols],
                gas_send.at[0],
                gas_recv.at[0, n],
                up,
            ),
            remote(
                ext.at[own, cols],
                ext.at[pl.ds(2 * rows, rows), cols],
                gas_send.at[1],
                gas_recv.at[1, n],
                down,
            ),
        )

    def both(up_step, down_step):
        pl.when(has_up)(up_step)
        pl.when(has_down)(down_step)

    def start_both(copies):
        both(copies[0].start, copies[1].start)

    def wait_both(copies):
        @pl.when(has_up)
        def _():
            copies[0].wait_send()
            copies[1].wait_recv()

        @pl.when(has_down)
        def _():
            copies[1].wait_send()
            copies[0].wait_recv()

    thirds = [pl.ds(n * rows, rows) for n in range(3)]

    def first_copy(d, third, src, where, sent):
        return remote(
            src, gz.at[d, thirds[third], :], first_send.at[d, sent], first_recv.at[d, third], where
        )

    head = pl.ds(0, lead)

    def first_own(d):
        return first_copy(d, 1, ext.at[own, head], {"sector": side[d]}, 1)

    def first_on(d, third):
        where = up if third == 0 else down
        return first_copy(d, third, gz.at[d, thirds[1], :], where, third)

    def first_seam(d, third):
        return first_copy(d, third, ext.at[thirds[third], head], {"sector": side[d]}, 2 - third)

    def on_seam(up_step, down_step):
        pl.when(seam_up)(up_step)
        pl.when(seam_down)(down_step)

    def off_seam(up_step, down_step):
        pl.when(jnp.logical_and(has_up, jnp.logical_not(seam_up)))(up_step)
        pl.when(jnp.logical_and(has_down, jnp.logical_not(seam_down)))(down_step)

    def arrive(copies):
        return copies[1].wait_recv, copies[0].wait_recv

    def leave(copies):
        return copies[0].start, copies[1].start

    first_col, count = pieces[whole]
    straight = (first_col, count // 2)
    around = pl.ds(first_col + count // 2, count // 2)
    out_up = remote(
        ext.at[own, around], hop, gas_send.at[0], hop_sem.at[0], {"band": bands - 1}
    )
    out_down = remote(ext.at[own, around], hop, gas_send.at[1], hop_sem.at[0], {"band": 0})
    on_up = remote(
        hop, ext.at[pl.ds(0, rows), around], hop_sem.at[1], hop_sem.at[2], {"band": bands // 2}
    )
    on_down = remote(
        hop,
        ext.at[pl.ds(2 * rows, rows), around],
        hop_sem.at[1],
        hop_sem.at[2],
        {"band": bands // 2 - 1},
    )

    on_seam(*leave(gas_copies(whole + 1)))
    on_seam(out_up.start, out_down.start)
    for n in range(whole):
        start_both(gas_copies(n))
    for d in range(2):
        first_own(d).start()
    on_seam(*leave(gas_copies(whole, straight)))
    off_seam(*leave(gas_copies(whole)))
    off_seam(*leave(gas_copies(whole + 1)))

    top = pl.ds(rows, 8)
    bottom = pl.ds(8, 8)
    halo_low = pl.ds(0, 8)
    halo_high = pl.ds(rows + 8, 8)
    drow = (
        remote(fld.at[:, top, :], fld.at[:, halo_low, :], row_send.at[0], row_recv.at[0], up),
        remote(fld.at[:, bottom, :], fld.at[:, halo_high, :], row_send.at[1], row_recv.at[1], down),
    )
    prow = (
        remote(prow_out.at[0], prow_in.at[0], row_send.at[2], row_recv.at[2], up),
        remote(prow_out.at[1], prow_in.at[1], row_send.at[3], row_recv.at[3], down),
    )

    @pl.when(jnp.logical_not(has_down))
    def _():
        ext[0:rows, :] = jnp.zeros((rows, arc), BF16)
        gz[:, 0:rows, :] = jnp.zeros((2, rows, lead), BF16)
        fld[:, 0:8, :] = jnp.zeros((3, 8, arc), F32)
        prow_in[0] = jnp.zeros((8, arc), F32)

    @pl.when(jnp.logical_not(has_up))
    def _():
        ext[2 * rows : 3 * rows, :] = jnp.zeros((rows, arc), BF16)
        gz[:, 2 * rows : 3 * rows, :] = jnp.zeros((2, rows, lead), BF16)
        fld[:, rows + 8 : rows + 16, :] = jnp.zeros((3, 8, arc), F32)
        prow_in[1] = jnp.zeros((8, arc), F32)

    def col_copy(kind, d):
        where = side_two[d] if kind == 2 else side[d]
        return remote(
            col_out.at[kind, d],
            col_in.at[kind, d],
            col_send.at[d],
            col_recv.at[kind, d],
            {"sector": where},
        )

    def edge(tile, d):
        lane = 127 if d == 0 else 0
        return jnp.transpose(tile)[lane : lane + 1, :]

    def edge_tile(d):
        return slice(arc - 128, arc) if d == 0 else slice(0, 128)

    for copy in load_fields:
        copy.wait()
    for d in range(2):
        for n in range(3):
            col_out[0, d, n : n + 1, :] = edge(fld[n, 8 : 8 + rows, edge_tile(d)], d)
        col_copy(0, d).start()

    def far_copy(d, n):
        if n < whole:
            part, cols = pl.ds(0, rows), pl.ds(*pieces[n])
        else:
            part, cols = pl.ds((n - whole) * chunk, chunk), pl.ds(*pieces[whole])
        return remote(
            far_out.at[d, part, cols],
            far_in.at[d, part, cols],
            far_send.at[d],
            far_recv.at[d, n],
            {"sector": side[d]},
        )

    rim = 16

    def span(c):
        if c >= chunks:
            return (0, rim) if c == chunks else (rows - rim, rim)
        low = c * chunk + (rim if c == 0 else 0)
        return low, (c + 1) * chunk - (rim if c == chunks - 1 else 0) - low

    def part_copy(d, c):
        part = pl.ds(*span(c))
        return remote(
            part_out.at[d, part, :],
            part_in.at[d, part, :],
            part_send.at[d],
            part_recv.at[d, min(c, chunks)],
            {"sector": side[d]},
        )

    order = [(chunks - n) % chunks for n in range(chunks)]
    load_gr[4].wait()
    load_gr[0].wait()
    def pass_on():
        for d in range(2):
            first_own(d).wait()
            off_seam(first_on(d, 0).start, first_on(d, 2).start)

    early = jnp.logical_or(lax.rem(band, 2) == 1, seam_down)
    pl.when(early)(pass_on)
    on_seam(*arrive(gas_copies(whole + 1)))
    for d in range(2):
        on_seam(first_seam(d, 2).start, first_seam(d, 0).start)

    for n in range(whole):
        both(*arrive(gas_copies(n)))
        cols = slice(pieces[n][0], pieces[n][0] + pieces[n][1])
        for d, j in ((0, 4), (1, 0)):
            far_out[d, :, cols] = jnp.dot(
                gr[j], ext[:, cols], preferred_element_type=F32
            ).astype(BF16)
            far_copy(d, n).start()
    pl.when(jnp.logical_not(early))(pass_on)
    @pl.when(band == bands - 1)
    def _():
        out_up.wait_recv()
        on_up.start()

    @pl.when(band == 0)
    def _():
        out_down.wait_recv()
        on_down.start()

    off_seam(*arrive(gas_copies(whole)))
    on_seam(*arrive(gas_copies(whole, straight)))
    on_seam(on_down.wait_recv, on_up.wait_recv)
    last = slice(pieces[whole][0], pieces[whole][0] + pieces[whole][1])
    for c in order:
        part = slice(c * chunk, (c + 1) * chunk)
        for d, j in ((0, 4), (1, 0)):
            far_out[d, part, last] = jnp.dot(
                gr[j, part, :], ext[:, last], preferred_element_type=F32
            ).astype(BF16)
            far_copy(d, whole + c).start()

    start_both(drow)
    off_seam(*arrive(gas_copies(whole + 1)))
    load_inner.wait()
    load_ga.wait()
    for d, j in ((0, 3), (1, 1)):
        near[d] = jnp.dot(gr[j], ext[...], preferred_element_type=F32).astype(BF16)

    for d, j in ((0, 4), (1, 0)):

        @pl.when(has_up)
        def _():
            first_on(d, 0).wait_send()
            first_on(d, 2).wait_recv()

        @pl.when(has_down)
        def _():
            first_on(d, 2).wait_send()
            first_on(d, 0).wait_recv()

        far_in[d, :, 0:lead] = jnp.dot(gr[j], gz[d], preferred_element_type=F32).astype(BF16)
    for d in range(2):
        for n in range(whole):
            far_copy(d, n).wait_recv()
    for c in order:
        part = slice(c * chunk, (c + 1) * chunk)
        for d, j in ((0, 3), (1, 1)):
            far_copy(d, whole + c).wait_recv()
            total = jnp.dot(near[d, part, :], ga[j], preferred_element_type=F32) + jnp.dot(
                far_in[d, part, :], ga[4 - 4 * d], preferred_element_type=F32
            )
            part_out[d, part, :] = total.astype(BF16)
            if c == 0:
                part_copy(d, chunks).start()
            if c == chunks - 1:
                part_copy(d, chunks + 1).start()
            part_copy(d, c).start()

    for d in range(2):
        col_out[2, d, 0:1, :] = edge(part_out[d, :, edge_tile(d)].astype(F32), d)
        col_copy(2, d).start()
        col_own[1 - d, 0:1, :] = edge(part_out[d, :, edge_tile(1 - d)].astype(F32), 1 - d)

    middle = jnp.dot(gr[2], ext[...], preferred_element_type=F32).astype(BF16)
    mid_pot[...] = jnp.dot(middle, ga[2], preferred_element_type=F32)
    for d in range(2):
        col_out[1, d, 0:1, :] = edge(mid_pot[:, edge_tile(d)], d)
        col_copy(1, d).start()

    load_k.wait()
    for d in range(2):
        col_copy(0, d).wait_recv()
    wait_both(drow)

    def columns(block):
        return jnp.transpose(jnp.concatenate([block, jnp.zeros((120, rows), F32)], axis=0))

    for d in range(2):
        dcol[d] = columns(col_in[0, d])

    def dust(start, stop):
        lanes = lax.broadcasted_iota(jnp.int32, (strip, arc), 1)
        is_first = lanes == 0
        is_last = lanes == arc - 1

        @pl.loop(start // strip, stop // strip)
        def _(step):
            first = pl.multiple_of(step * strip, strip)
            part = pl.ds(first, strip)
            window = pl.ds(first, strip + 16)
            inv = inverse_radius(band * rows + first, strip, rows * bands)
            west_edge = dcol[0, part, :]
            east_edge = dcol[1, part, :]
            centre, above, below, east, west = [], [], [], [], []
            for n in range(3):
                q = fld[n, window, :]
                mid = q[8 : 8 + strip]
                centre.append(mid)
                above.append(q[9 : 9 + strip])
                below.append(q[7 : 7 + strip])
                east.append(
                    jnp.where(is_last, east_edge[:, n : n + 1], pltpu.roll(mid, arc - 1, 1))
                )
                west.append(jnp.where(is_first, west_edge[:, n : n + 1], pltpu.roll(mid, 1, 1)))
            rho, u, w = centre
            k = kv[part, :].astype(F32)
            lap = [above[n] + below[n] + east[n] + west[n] - 4.0 * centre[n] for n in range(3)]
            density_next[part, :] = (
                rho
                - 0.5 * (above[0] * above[1] - below[0] * below[1])
                - 0.5 * inv * (east[0] * east[2] - west[0] * west[2])
                + diffusion * lap[0]
            )
            radial_next[part, :] = (
                u
                - 0.5 * u * (above[1] - below[1])
                - 0.5 * inv * w * (east[1] - west[1])
                - k * u
                + diffusion * lap[1]
            )
            azimuth_next[part, :] = (
                w
                - 0.5 * u * (above[2] - below[2])
                - 0.5 * inv * w * (east[2] - west[2])
                - k * (w - kepler * jnp.sqrt(inv))
                + diffusion * lap[2]
            )

    def settled(low):
        part = slice(low, low + rim)
        return mid_pot[part, :] + (
            part_in[0, part, :].astype(F32) + part_in[1, part, :].astype(F32)
        )

    for d in range(2):
        both_rims = pl.ds(0, 2 * rim)
        remote(
            part_out.at[d, both_rims, :],
            part_in.at[d, both_rims, :],
            part_send.at[d],
            part_recv.at[d, chunks],
            {"sector": side[d]},
        ).wait_recv()
    prow_out[1] = settled(0)[0:8]
    prow_out[0] = settled(rows - rim)[rim - 8 : rim]
    start_both(prow)

    dust(0, rows)

    for d in range(2):
        col_copy(1, d).wait_recv()
        col_copy(2, d).wait_recv()
        row = col_in[1, d, 0:1, :] + (col_in[2, d, 0:1, :] + col_own[d, 0:1, :])
        edges[d] = jnp.transpose(jnp.concatenate([row, jnp.zeros((127, rows), F32)], axis=0))

    for c in order:
        for d in range(2):
            part_copy(d, c).wait_recv()
    wait_both(prow)
    rims[...] = prow_in[...]

    pl.when(band == bands - 1)(on_up.wait_send)
    pl.when(band == 0)(on_down.wait_send)
    sent_cols = pl.ds(lead, arc - lead)
    for d in range(2):
        where = {"sector": side[d]}
        remote(
            far_out.at[d, :, sent_cols],
            far_in.at[d, :, sent_cols],
            far_send.at[d],
            far_recv.at[d, 0],
            where,
        ).wait_send()
        remote(
            part_out.at[d], part_in.at[d], part_send.at[d], part_recv.at[d, 0], where
        ).wait_send()
        remote(
            col_out.at[:, d], col_in.at[:, d], col_send.at[d], col_recv.at[0, d], where
        ).wait_send()
    both(
        remote(ext.at[own, :], ext.at[thirds[0], :], gas_send.at[0], gas_recv.at[0, 0], up).wait_send,
        remote(ext.at[own, :], ext.at[thirds[2], :], gas_send.at[1], gas_recv.at[1, 0], down).wait_send,
    )


def finish(
    chunk,
    mid_pot,
    parts,
    rims,
    edges,
    density_part,
    radial_part,
    azimuth_part,
    potential,
    density_next,
    radial_next,
    azimuth_next,
    potp,
    radial,
    azimuth,
    sem,
):
    rows, arc = density_part.shape
    band = lax.axis_index("band")
    total_rows = rows * lax.axis_size("band")
    chunks = rows // chunk
    copies = [pltpu.make_async_copy(density_part, density_next, sem.at[0])]
    copies[0].start()
    potp[0:8, :] = rims[0]
    potp[rows + 8 : rows + 16, :] = rims[1]
    for c in range(chunks):
        part = slice(c * chunk, (c + 1) * chunk)
        potp[8 + c * chunk : 8 + (c + 1) * chunk, :] = mid_pot[part, :] + (
            parts[0, part, :].astype(F32) + parts[1, part, :].astype(F32)
        )
        copies.append(
            pltpu.make_async_copy(
                potp.at[pl.ds(8 + c * chunk, chunk), :],
                potential.at[pl.ds(c * chunk, chunk), :],
                sem.at[1 + c],
            )
        )
        copies[-1].start()
    lanes = lax.broadcasted_iota(jnp.int32, (chunk, arc), 1)
    is_first = lanes == 0
    is_last = lanes == arc - 1
    for c in range(chunks):
        part = slice(c * chunk, (c + 1) * chunk)
        cut = pl.ds(c * chunk, chunk)
        q = potp[c * chunk : (c + 1) * chunk + 16, :]
        radial[part, :] = radial_part[part, :] - 0.5 * gravity * (
            q[9 : 9 + chunk] - q[7 : 7 + chunk]
        )
        copies.append(
            pltpu.make_async_copy(radial.at[cut, :], radial_next.at[cut, :], sem.at[1 + chunks + 2 * c])
        )
        copies[-1].start()
        mid = q[8 : 8 + chunk]
        inv = inverse_radius(band * rows + c * chunk, chunk, total_rows)
        east = jnp.where(is_last, edges[1, part, 0:1], pltpu.roll(mid, arc - 1, 1))
        west = jnp.where(is_first, edges[0, part, 0:1], pltpu.roll(mid, 1, 1))
        azimuth[part, :] = azimuth_part[part, :] - 0.5 * gravity * inv * (east - west)
        copies.append(
            pltpu.make_async_copy(azimuth.at[cut, :], azimuth_next.at[cut, :], sem.at[2 + chunks + 2 * c])
        )
        copies[-1].start()
    for copy in copies:
        copy.wait()


def body(gas, green_radial, green_azimuth, rho, u, w, coupling, chunk, strip, pieces):
    lead = pieces[-1][1]
    rows, arc = rho.shape
    chunks = rows // chunk
    steps = len(pieces)
    dma = pltpu.SemaphoreType.DMA
    operands = (gas, green_radial, green_azimuth, rho, u, w, coupling)
    results = pl.pallas_call(
        functools.partial(kernel, chunk, strip, pieces),
        out_shape=[
            pltpu.VMEM((rows, arc), F32),
            pltpu.VMEM((2, rows, arc), BF16),
            pltpu.VMEM((2, 8, arc), F32),
            pltpu.VMEM((2, rows, 128), F32),
        ]
        + [pltpu.VMEM((rows, arc), F32)] * 3,
        in_specs=[pl.BlockSpec(memory_space=pltpu.HBM)] * 7,
        out_specs=[pl.BlockSpec(memory_space=pltpu.VMEM)] * 7,
        scratch_shapes=[
            pltpu.VMEM((3 * rows, arc), BF16),
            pltpu.VMEM((2, 3 * rows, lead), BF16),
            pltpu.VMEM((rows, pieces[-2][1] // 2), BF16),
            pltpu.VMEM((5, rows, 3 * rows), BF16),
            pltpu.VMEM((5, arc, arc), BF16),
            pltpu.VMEM((3, rows + 16, arc), F32),
            pltpu.VMEM((rows, arc), BF16),
            pltpu.VMEM((2, 8, arc), F32),
            pltpu.VMEM((2, 8, arc), F32),
            pltpu.VMEM((2, rows, arc), BF16),
            pltpu.VMEM((2, rows, arc), BF16),
            pltpu.VMEM((2, rows, arc), BF16),
            pltpu.VMEM((2, rows, arc), BF16),
            pltpu.VMEM((3, 2, 8, rows), F32),
            pltpu.VMEM((3, 2, 8, rows), F32),
            pltpu.VMEM((2, 8, rows), F32),
            pltpu.VMEM((2, rows, 128), F32),
            dma((9,)),
            dma((2,)),
            dma((2, steps)),
            dma((2, 3)),
            dma((2, 3)),
            dma((3,)),
            dma((4,)),
            dma((4,)),
            dma((2,)),
            dma((3, 2)),
            dma((2,)),
            dma((2, steps - 2 + chunks)),
            dma((2,)),
            dma((2, chunks + 1)),
        ],
        compiler_params=pltpu.CompilerParams(
            collective_id=0, has_side_effects=True, vmem_limit_bytes=50 * 2**20
        ),
        name="disc",
    )(*[pltpu.with_memory_space_constraint(x, pltpu.HBM) for x in operands])
    return pl.pallas_call(
        functools.partial(finish, chunk),
        out_shape=[jax.ShapeDtypeStruct((rows, arc), F32)] * 4,
        in_specs=[pl.BlockSpec(memory_space=pltpu.VMEM)] * 7,
        out_specs=[pl.BlockSpec(memory_space=pl.ANY)] * 4,
        scratch_shapes=[
            pltpu.VMEM((rows + 16, arc), F32),
            pltpu.VMEM((rows, arc), F32),
            pltpu.VMEM((rows, arc), F32),
            dma((1 + 3 * chunks,)),
        ],
        compiler_params=pltpu.CompilerParams(vmem_limit_bytes=4 * 2**20),
        name="finish",
    )(*[pltpu.with_memory_space_constraint(r, pltpu.VMEM) for r in results])


def solution(mesh, chunk=96, strip=32, pieces=((128, 128), (256, 256), (0, 128))):
    return jax.shard_map(
        functools.partial(body, chunk=chunk, strip=strip, pieces=pieces),
        mesh=mesh,
        in_specs=(
            P("band", "sector"),
            P(None, "band", None),
            P(),
            P("band", "sector"),
            P("band", "sector"),
            P("band", "sector"),
            P("band", "sector"),
        ),
        out_specs=(P("band", "sector"),) * 4,
        check_vma=False,
    )
```

```python
import functools

import jax
import jax.numpy as jnp
from jax import lax
from jax.experimental import pallas as pl
from jax.experimental.pallas import tpu as pltpu
from jax.sharding import PartitionSpec as P

diffusion = 0.1
gravity = 0.1
kepler = 0.6

MESH = pl.DeviceIdType.MESH
F32 = jnp.float32
BF16 = jnp.bfloat16


def inverse_radius(first, count, total_rows):
    index = first + lax.broadcasted_iota(jnp.int32, (count, 1), 0)
    return 1.0 / (1.0 + 3.0 * (index.astype(F32) + 0.5) / total_rows)


def kernel(
    chunk,
    strip,
    pieces,
    gas,
    green_radial,
    green_azimuth,
    dust_density,
    dust_radial,
    dust_azimuth,
    coupling,
    mid_pot,
    part_in,
    rims,
    edges,
    density_next,
    radial_next,
    azimuth_next,
    ext,
    gz,
    hop,
    gr,
    ga,
    fld,
    kv,
    prow_out,
    prow_in,
    near,
    far_out,
    far_in,
    part_out,
    col_out,
    col_in,
    col_own,
    dcol,
    load_sem,
    gas_send,
    gas_recv,
    first_send,
    first_recv,
    hop_sem,
    row_send,
    row_recv,
    col_send,
    col_recv,
    far_send,
    far_recv,
    part_send,
    part_recv,
):
    rows, arc = dust_density.shape
    chunks = rows // chunk
    band = lax.axis_index("band")
    sector = lax.axis_index("sector")
    bands = lax.axis_size("band")
    sectors = lax.axis_size("sector")
    side = (lax.rem(sector + 1, sectors), lax.rem(sector + sectors - 1, sectors))
    side_two = (lax.rem(sector + 2, sectors), lax.rem(sector + sectors - 2, sectors))
    has_up = band < bands - 1
    has_down = band > 0
    seam_up = band == bands // 2 - 1
    seam_down = band == bands // 2
    seam = jnp.logical_or(seam_up, seam_down)
    end = jnp.logical_or(band == 0, band == bands - 1)

    lead = gz.shape[2]
    whole = len(pieces) - 2

    barrier = pltpu.get_barrier_semaphore()
    for s in side + side_two:
        pl.semaphore_signal(barrier, inc=1, device_id={"sector": s}, device_id_type=MESH)

    @pl.when(has_up)
    def _():
        pl.semaphore_signal(barrier, inc=1, device_id={"band": band + 1}, device_id_type=MESH)

    @pl.when(has_down)
    def _():
        pl.semaphore_signal(barrier, inc=1, device_id={"band": band - 1}, device_id_type=MESH)

    @pl.when(seam)
    def _():
        for b in (0, bands - 1):
            pl.semaphore_signal(barrier, inc=1, device_id={"band": b}, device_id_type=MESH)

    @pl.when(end)
    def _():
        for b in (bands // 2 - 1, bands // 2):
            pl.semaphore_signal(barrier, inc=1, device_id={"band": b}, device_id_type=MESH)

    def load(src, dst, n):
        copy = pltpu.make_async_copy(src, dst, load_sem.at[n])
        copy.start()
        return copy

    own = pl.ds(rows, rows)
    body_rows = pl.ds(8, rows)
    load_gas = load(gas, ext.at[own, :], 3)
    load_gr = {}
    for n, j in enumerate((4, 0)):
        load_gr[j] = load(green_radial.at[j], gr.at[n], 4 + n)
    load_fields = [
        load(field, fld.at[n, body_rows, :], n)
        for n, field in enumerate((dust_density, dust_radial, dust_azimuth))
    ]
    load_inner = [
        load(green_radial.at[j], gr.at[n], m) for j, n, m in ((3, 2, 6), (1, 3, 9), (2, 4, 10))
    ]
    load_ga = load(green_azimuth, ga, 7)
    load_k = load(coupling, kv, 8)

    load_gas.wait()
    pl.semaphore_wait(
        barrier,
        4
        + has_up.astype(jnp.int32)
        + has_down.astype(jnp.int32)
        + 2 * seam.astype(jnp.int32)
        + 2 * end.astype(jnp.int32),
    )

    def remote(src, dst, send, recv, where):
        return pltpu.make_async_remote_copy(
            src_ref=src,
            dst_ref=dst,
            send_sem=send,
            recv_sem=recv,
            device_id=where,
            device_id_type=MESH,
        )

    up = {"band": band + 1}
    down = {"band": band - 1}

    def gas_copies(n, part=None):
        cols = pl.ds(*(part or pieces[n]))
        return (
            remote(
                ext.at[own, cols],
                ext.at[pl.ds(0, rows), cols],
                gas_send.at[0],
                gas_recv.at[0, n],
                up,
            ),
            remote(
                ext.at[own, cols],
                ext.at[pl.ds(2 * rows, rows), cols],
                gas_send.at[1],
                gas_recv.at[1, n],
                down,
            ),
        )

    def both(up_step, down_step):
        pl.when(has_up)(up_step)
        pl.when(has_down)(down_step)

    def start_both(copies):
        both(copies[0].start, copies[1].start)

    def wait_both(copies):
        @pl.when(has_up)
        def _():
            copies[0].wait_send()
            copies[1].wait_recv()

        @pl.when(has_down)
        def _():
            copies[1].wait_send()
            copies[0].wait_recv()

    thirds = [pl.ds(n * rows, rows) for n in range(3)]

    def first_copy(d, third, src, where, sent):
        return remote(
            src, gz.at[d, thirds[third], :], first_send.at[d, sent], first_recv.at[d, third], where
        )

    head = pl.ds(0, lead)

    def first_own(d):
        return first_copy(d, 1, ext.at[own, head], {"sector": side[d]}, 1)

    def first_on(d, third):
        where = up if third == 0 else down
        return first_copy(d, third, gz.at[d, thirds[1], :], where, third)

    def first_seam(d, third):
        return first_copy(d, third, ext.at[thirds[third], head], {"sector": side[d]}, 2 - third)

    def on_seam(up_step, down_step):
        pl.when(seam_up)(up_step)
        pl.when(seam_down)(down_step)

    def off_seam(up_step, down_step):
        pl.when(jnp.logical_and(has_up, jnp.logical_not(seam_up)))(up_step)
        pl.when(jnp.logical_and(has_down, jnp.logical_not(seam_down)))(down_step)

    def arrive(copies):
        return copies[1].wait_recv, copies[0].wait_recv

    def leave(copies):
        return copies[0].start, copies[1].start

    first_col, count = pieces[whole]
    straight = (first_col, count // 2)
    around = pl.ds(first_col + count // 2, count // 2)
    out_up = remote(
        ext.at[own, around], hop, gas_send.at[0], hop_sem.at[0], {"band": bands - 1}
    )
    out_down = remote(ext.at[own, around], hop, gas_send.at[1], hop_sem.at[0], {"band": 0})
    on_up = remote(
        hop, ext.at[pl.ds(0, rows), around], hop_sem.at[1], hop_sem.at[2], {"band": bands // 2}
    )
    on_down = remote(
        hop,
        ext.at[pl.ds(2 * rows, rows), around],
        hop_sem.at[1],
        hop_sem.at[2],
        {"band": bands // 2 - 1},
    )

    on_seam(*leave(gas_copies(whole + 1)))
    on_seam(out_up.start, out_down.start)
    for n in range(whole):
        start_both(gas_copies(n))
    for d in range(2):
        first_own(d).start()
    on_seam(*leave(gas_copies(whole, straight)))
    off_seam(*leave(gas_copies(whole)))
    off_seam(*leave(gas_copies(whole + 1)))

    top = pl.ds(rows, 8)
    bottom = pl.ds(8, 8)
    halo_low = pl.ds(0, 8)
    halo_high = pl.ds(rows + 8, 8)
    drow = (
        remote(fld.at[:, top, :], fld.at[:, halo_low, :], row_send.at[0], row_recv.at[0], up),
        remote(fld.at[:, bottom, :], fld.at[:, halo_high, :], row_send.at[1], row_recv.at[1], down),
    )
    prow = (
        remote(prow_out.at[0], prow_in.at[0], row_send.at[2], row_recv.at[2], up),
        remote(prow_out.at[1], prow_in.at[1], row_send.at[3], row_recv.at[3], down),
    )

    @pl.when(jnp.logical_not(has_down))
    def _():
        ext[0:rows, :] = jnp.zeros((rows, arc), BF16)
        gz[:, 0:rows, :] = jnp.zeros((2, rows, lead), BF16)
        fld[:, 0:8, :] = jnp.zeros((3, 8, arc), F32)
        prow_in[0] = jnp.zeros((8, arc), F32)

    @pl.when(jnp.logical_not(has_up))
    def _():
        ext[2 * rows : 3 * rows, :] = jnp.zeros((rows, arc), BF16)
        gz[:, 2 * rows : 3 * rows, :] = jnp.zeros((2, rows, lead), BF16)
        fld[:, rows + 8 : rows + 16, :] = jnp.zeros((3, 8, arc), F32)
        prow_in[1] = jnp.zeros((8, arc), F32)

    def col_copy(kind, d):
        where = side_two[d] if kind == 2 else side[d]
        return remote(
            col_out.at[kind, d],
            col_in.at[kind, d],
            col_send.at[d],
            col_recv.at[kind, d],
            {"sector": where},
        )

    def edge(tile, d):
        lane = 127 if d == 0 else 0
        return jnp.transpose(tile)[lane : lane + 1, :]

    def edge_tile(d):
        return slice(arc - 128, arc) if d == 0 else slice(0, 128)

    for copy in load_fields:
        copy.wait()
    for d in range(2):
        for n in range(3):
            col_out[0, d, n : n + 1, :] = edge(fld[n, 8 : 8 + rows, edge_tile(d)], d)
        col_copy(0, d).start()

    def far_copy(d, n):
        if n < whole:
            part, cols = pl.ds(0, rows), pl.ds(*pieces[n])
        else:
            part, cols = pl.ds((n - whole) * chunk, chunk), pl.ds(*pieces[whole])
        return remote(
            far_out.at[d, part, cols],
            far_in.at[d, part, cols],
            far_send.at[d],
            far_recv.at[d, n],
            {"sector": side[d]},
        )

    rim = 16

    def span(c):
        if c >= chunks:
            return (0, rim) if c == chunks else (rows - rim, rim)
        low = c * chunk + (rim if c == 0 else 0)
        return low, (c + 1) * chunk - (rim if c == chunks - 1 else 0) - low

    def part_copy(d, c):
        part = pl.ds(*span(c))
        return remote(
            part_out.at[d, part, :],
            part_in.at[d, part, :],
            part_send.at[d],
            part_recv.at[d, min(c, chunks)],
            {"sector": side[d]},
        )

    order = [(chunks - n) % chunks for n in range(chunks)]
    load_gr[4].wait()
    load_gr[0].wait()
    def pass_on():
        for d in range(2):
            first_own(d).wait()
            off_seam(first_on(d, 0).start, first_on(d, 2).start)

    early = jnp.logical_or(lax.rem(band, 2) == 1, seam_down)
    pl.when(early)(pass_on)
    on_seam(*arrive(gas_copies(whole + 1)))
    for d in range(2):
        on_seam(first_seam(d, 2).start, first_seam(d, 0).start)

    for n in range(whole):
        both(*arrive(gas_copies(n)))
        cols = slice(pieces[n][0], pieces[n][0] + pieces[n][1])
        for d, j in ((0, 4), (1, 0)):
            far_out[d, :, cols] = jnp.dot(
                gr[d], ext[:, cols], preferred_element_type=F32
            ).astype(BF16)
            far_copy(d, n).start()
    pl.when(jnp.logical_not(early))(pass_on)
    @pl.when(band == bands - 1)
    def _():
        out_up.wait_recv()
        on_up.start()

    @pl.when(band == 0)
    def _():
        out_down.wait_recv()
        on_down.start()

    off_seam(*arrive(gas_copies(whole)))
    on_seam(*arrive(gas_copies(whole, straight)))
    on_seam(on_down.wait_recv, on_up.wait_recv)
    last = slice(pieces[whole][0], pieces[whole][0] + pieces[whole][1])
    for c in order:
        part = slice(c * chunk, (c + 1) * chunk)
        pair = jnp.dot(
            gr[0:2, part, :].reshape(2 * chunk, 3 * rows),
            ext[:, last],
            preferred_element_type=F32,
        ).astype(BF16)
        for d in range(2):
            far_out[d, part, last] = pair[d * chunk : (d + 1) * chunk]
            far_copy(d, whole + c).start()

    start_both(drow)
    off_seam(*arrive(gas_copies(whole + 1)))
    for copy in load_inner:
        copy.wait()
    load_ga.wait()
    pair = jnp.dot(
        gr[2:4].reshape(2 * rows, 3 * rows), ext[...], preferred_element_type=F32
    ).astype(BF16)
    for d in range(2):
        near[d] = pair[d * rows : (d + 1) * rows]

    for d, j in ((0, 4), (1, 0)):

        @pl.when(has_up)
        def _():
            first_on(d, 0).wait_send()
            first_on(d, 2).wait_recv()

        @pl.when(has_down)
        def _():
            first_on(d, 2).wait_send()
            first_on(d, 0).wait_recv()

        far_in[d, :, 0:lead] = jnp.dot(gr[d], gz[d], preferred_element_type=F32).astype(BF16)
    for d in range(2):
        for n in range(whole):
            far_copy(d, n).wait_recv()
    for c in order:
        part = slice(c * chunk, (c + 1) * chunk)
        for d, j in ((0, 3), (1, 1)):
            far_copy(d, whole + c).wait_recv()
            total = jnp.dot(near[d, part, :], ga[j], preferred_element_type=F32) + jnp.dot(
                far_in[d, part, :], ga[4 - 4 * d], preferred_element_type=F32
            )
            part_out[d, part, :] = total.astype(BF16)
            if c == 0:
                part_copy(d, chunks).start()
            if c == chunks - 1:
                part_copy(d, chunks + 1).start()
            part_copy(d, c).start()

    for d in range(2):
        col_out[2, d, 0:1, :] = edge(part_out[d, :, edge_tile(d)].astype(F32), d)
        col_copy(2, d).start()
        col_own[1 - d, 0:1, :] = edge(part_out[d, :, edge_tile(1 - d)].astype(F32), 1 - d)

    middle = jnp.dot(gr[4], ext[...], preferred_element_type=F32).astype(BF16)
    mid_pot[...] = jnp.dot(middle, ga[2], preferred_element_type=F32)
    for d in range(2):
        col_out[1, d, 0:1, :] = edge(mid_pot[:, edge_tile(d)], d)
        col_copy(1, d).start()

    load_k.wait()
    for d in range(2):
        col_copy(0, d).wait_recv()
    wait_both(drow)

    def columns(block):
        return jnp.transpose(jnp.concatenate([block, jnp.zeros((120, rows), F32)], axis=0))

    for d in range(2):
        dcol[d] = columns(col_in[0, d])

    def dust(start, stop):
        lanes = lax.broadcasted_iota(jnp.int32, (strip, arc), 1)
        is_first = lanes == 0
        is_last = lanes == arc - 1

        @pl.loop(start // strip, stop // strip)
        def _(step):
            first = pl.multiple_of(step * strip, strip)
            part = pl.ds(first, strip)
            window = pl.ds(first, strip + 16)
            inv = inverse_radius(band * rows + first, strip, rows * bands)
            west_edge = dcol[0, part, :]
            east_edge = dcol[1, part, :]
            centre, above, below, east, west = [], [], [], [], []
            for n in range(3):
                q = fld[n, window, :]
                mid = q[8 : 8 + strip]
                centre.append(mid)
                above.append(q[9 : 9 + strip])
                below.append(q[7 : 7 + strip])
                east.append(
                    jnp.where(is_last, east_edge[:, n : n + 1], pltpu.roll(mid, arc - 1, 1))
                )
                west.append(jnp.where(is_first, west_edge[:, n : n + 1], pltpu.roll(mid, 1, 1)))
            rho, u, w = centre
            k = kv[part, :].astype(F32)
            lap = [above[n] + below[n] + east[n] + west[n] - 4.0 * centre[n] for n in range(3)]
            density_next[part, :] = (
                rho
                - 0.5 * (above[0] * above[1] - below[0] * below[1])
                - 0.5 * inv * (east[0] * east[2] - west[0] * west[2])
                + diffusion * lap[0]
            )
            radial_next[part, :] = (
                u
                - 0.5 * u * (above[1] - below[1])
                - 0.5 * inv * w * (east[1] - west[1])
                - k * u
                + diffusion * lap[1]
            )
            azimuth_next[part, :] = (
                w
                - 0.5 * u * (above[2] - below[2])
                - 0.5 * inv * w * (east[2] - west[2])
                - k * (w - kepler * jnp.sqrt(inv))
                + diffusion * lap[2]
            )

    def settled(low):
        part = slice(low, low + rim)
        return mid_pot[part, :] + (
            part_in[0, part, :].astype(F32) + part_in[1, part, :].astype(F32)
        )

    for d in range(2):
        both_rims = pl.ds(0, 2 * rim)
        remote(
            part_out.at[d, both_rims, :],
            part_in.at[d, both_rims, :],
            part_send.at[d],
            part_recv.at[d, chunks],
            {"sector": side[d]},
        ).wait_recv()
    prow_out[1] = settled(0)[0:8]
    prow_out[0] = settled(rows - rim)[rim - 8 : rim]
    start_both(prow)

    dust(0, rows)

    for d in range(2):
        col_copy(1, d).wait_recv()
        col_copy(2, d).wait_recv()
        row = col_in[1, d, 0:1, :] + (col_in[2, d, 0:1, :] + col_own[d, 0:1, :])
        edges[d] = jnp.transpose(jnp.concatenate([row, jnp.zeros((127, rows), F32)], axis=0))

    for c in order:
        for d in range(2):
            part_copy(d, c).wait_recv()
    wait_both(prow)
    rims[...] = prow_in[...]

    pl.when(band == bands - 1)(on_up.wait_send)
    pl.when(band == 0)(on_down.wait_send)
    sent_cols = pl.ds(lead, arc - lead)
    for d in range(2):
        where = {"sector": side[d]}
        remote(
            far_out.at[d, :, sent_cols],
            far_in.at[d, :, sent_cols],
            far_send.at[d],
            far_recv.at[d, 0],
            where,
        ).wait_send()
        remote(
            part_out.at[d], part_in.at[d], part_send.at[d], part_recv.at[d, 0], where
        ).wait_send()
        remote(
            col_out.at[:, d], col_in.at[:, d], col_send.at[d], col_recv.at[0, d], where
        ).wait_send()
    both(
        remote(ext.at[own, :], ext.at[thirds[0], :], gas_send.at[0], gas_recv.at[0, 0], up).wait_send,
        remote(ext.at[own, :], ext.at[thirds[2], :], gas_send.at[1], gas_recv.at[1, 0], down).wait_send,
    )


def finish(
    chunk,
    mid_pot,
    parts,
    rims,
    edges,
    density_part,
    radial_part,
    azimuth_part,
    potential,
    density_next,
    radial_next,
    azimuth_next,
    potp,
    radial,
    azimuth,
    sem,
):
    rows, arc = density_part.shape
    band = lax.axis_index("band")
    total_rows = rows * lax.axis_size("band")
    chunks = rows // chunk
    copies = [pltpu.make_async_copy(density_part, density_next, sem.at[0])]
    copies[0].start()
    potp[0:8, :] = rims[0]
    potp[rows + 8 : rows + 16, :] = rims[1]
    for c in range(chunks):
        part = slice(c * chunk, (c + 1) * chunk)
        potp[8 + c * chunk : 8 + (c + 1) * chunk, :] = mid_pot[part, :] + (
            parts[0, part, :].astype(F32) + parts[1, part, :].astype(F32)
        )
        copies.append(
            pltpu.make_async_copy(
                potp.at[pl.ds(8 + c * chunk, chunk), :],
                potential.at[pl.ds(c * chunk, chunk), :],
                sem.at[1 + c],
            )
        )
        copies[-1].start()
    lanes = lax.broadcasted_iota(jnp.int32, (chunk, arc), 1)
    is_first = lanes == 0
    is_last = lanes == arc - 1
    for c in range(chunks):
        part = slice(c * chunk, (c + 1) * chunk)
        cut = pl.ds(c * chunk, chunk)
        q = potp[c * chunk : (c + 1) * chunk + 16, :]
        radial[part, :] = radial_part[part, :] - 0.5 * gravity * (
            q[9 : 9 + chunk] - q[7 : 7 + chunk]
        )
        copies.append(
            pltpu.make_async_copy(radial.at[cut, :], radial_next.at[cut, :], sem.at[1 + chunks + 2 * c])
        )
        copies[-1].start()
        mid = q[8 : 8 + chunk]
        inv = inverse_radius(band * rows + c * chunk, chunk, total_rows)
        east = jnp.where(is_last, edges[1, part, 0:1], pltpu.roll(mid, arc - 1, 1))
        west = jnp.where(is_first, edges[0, part, 0:1], pltpu.roll(mid, 1, 1))
        azimuth[part, :] = azimuth_part[part, :] - 0.5 * gravity * inv * (east - west)
        copies.append(
            pltpu.make_async_copy(azimuth.at[cut, :], azimuth_next.at[cut, :], sem.at[2 + chunks + 2 * c])
        )
        copies[-1].start()
    for copy in copies:
        copy.wait()


def body(gas, green_radial, green_azimuth, rho, u, w, coupling, chunk, strip, pieces):
    lead = pieces[-1][1]
    rows, arc = rho.shape
    chunks = rows // chunk
    steps = len(pieces)
    dma = pltpu.SemaphoreType.DMA
    operands = (gas, green_radial, green_azimuth, rho, u, w, coupling)
    results = pl.pallas_call(
        functools.partial(kernel, chunk, strip, pieces),
        out_shape=[
            pltpu.VMEM((rows, arc), F32),
            pltpu.VMEM((2, rows, arc), BF16),
            pltpu.VMEM((2, 8, arc), F32),
            pltpu.VMEM((2, rows, 128), F32),
        ]
        + [pltpu.VMEM((rows, arc), F32)] * 3,
        in_specs=[pl.BlockSpec(memory_space=pltpu.HBM)] * 7,
        out_specs=[pl.BlockSpec(memory_space=pltpu.VMEM)] * 7,
        scratch_shapes=[
            pltpu.VMEM((3 * rows, arc), BF16),
            pltpu.VMEM((2, 3 * rows, lead), BF16),
            pltpu.VMEM((rows, pieces[-2][1] // 2), BF16),
            pltpu.VMEM((5, rows, 3 * rows), BF16),
            pltpu.VMEM((5, arc, arc), BF16),
            pltpu.VMEM((3, rows + 16, arc), F32),
            pltpu.VMEM((rows, arc), BF16),
            pltpu.VMEM((2, 8, arc), F32),
            pltpu.VMEM((2, 8, arc), F32),
            pltpu.VMEM((2, rows, arc), BF16),
            pltpu.VMEM((2, rows, arc), BF16),
            pltpu.VMEM((2, rows, arc), BF16),
            pltpu.VMEM((2, rows, arc), BF16),
            pltpu.VMEM((3, 2, 8, rows), F32),
            pltpu.VMEM((3, 2, 8, rows), F32),
            pltpu.VMEM((2, 8, rows), F32),
            pltpu.VMEM((2, rows, 128), F32),
            dma((11,)),
            dma((2,)),
            dma((2, steps)),
            dma((2, 3)),
            dma((2, 3)),
            dma((3,)),
            dma((4,)),
            dma((4,)),
            dma((2,)),
            dma((3, 2)),
            dma((2,)),
            dma((2, steps - 2 + chunks)),
            dma((2,)),
            dma((2, chunks + 1)),
        ],
        compiler_params=pltpu.CompilerParams(
            collective_id=0, has_side_effects=True, vmem_limit_bytes=50 * 2**20
        ),
        name="disc",
    )(*[pltpu.with_memory_space_constraint(x, pltpu.HBM) for x in operands])
    return pl.pallas_call(
        functools.partial(finish, chunk),
        out_shape=[jax.ShapeDtypeStruct((rows, arc), F32)] * 4,
        in_specs=[pl.BlockSpec(memory_space=pltpu.VMEM)] * 7,
        out_specs=[pl.BlockSpec(memory_space=pl.ANY)] * 4,
        scratch_shapes=[
            pltpu.VMEM((rows + 16, arc), F32),
            pltpu.VMEM((rows, arc), F32),
            pltpu.VMEM((rows, arc), F32),
            dma((1 + 3 * chunks,)),
        ],
        compiler_params=pltpu.CompilerParams(vmem_limit_bytes=4 * 2**20),
        name="finish",
    )(*[pltpu.with_memory_space_constraint(r, pltpu.VMEM) for r in results])


def solution(mesh, chunk=96, strip=32, pieces=((128, 128), (256, 256), (0, 128))):
    return jax.shard_map(
        functools.partial(body, chunk=chunk, strip=strip, pieces=pieces),
        mesh=mesh,
        in_specs=(
            P("band", "sector"),
            P(None, "band", None),
            P(),
            P("band", "sector"),
            P("band", "sector"),
            P("band", "sector"),
            P("band", "sector"),
        ),
        out_specs=(P("band", "sector"),) * 4,
        check_vma=False,
    )
```
